32 devices in a mesh: groups: 2 (over y), fsdp: 8 (over z, x), section: 2 (over core).
Axes of the slice: x: 2, y: 2, z: 4, core: 2. Of those that a mesh axis runs over, the one named last changes fastest.
Arguments:
- tokens: bfloat16 [512, 8192], P(('groups', 'section'), 'fsdp'), parts along dimension 0, may hold values from -6 to 6
- cotangent: bfloat16 [512, 8192], P(('groups', 'section'), 'fsdp'), parts along dimension 0, may hold values from -6 to 6
- gate_blocks: bfloat16 [128, 128, 128], P('fsdp'), may hold values from -0.125 to 0.125
- up_blocks: bfloat16 [128, 128, 128], P('fsdp'), may hold values from -0.125 to 0.125
- down_blocks: bfloat16 [128, 128, 128], P('fsdp'), may hold values from -0.125 to 0.125
- gate_dest: int32 [128, 1], P('fsdp'), may hold values from 0 to 7; in each aligned block of 16 rows (0 to 15, 16 to 31, ...) at most 3 rows name the same one
- up_dest: int32 [128, 1], P('fsdp'), may hold values from 0 to 7; in each aligned block of 16 rows (0 to 15, 16 to 31, ...) at most 3 rows name the same one
- down_dest: int32 [128, 1], P('fsdp'), may hold values from 0 to 7; in each aligned block of 16 rows (0 to 15, 16 to 31, ...) at most 3 rows name the same one
- gate_rows: int32 [128], P('fsdp'), may hold values from 0 to 63
- up_rows: int32 [128], P('fsdp'), may hold values from 0 to 63
- down_rows: int32 [128], P('fsdp'), may hold values from 0 to 63
Outputs:
- input_grad: bfloat16 [512, 8192], P(('groups', 'section'), 'fsdp'), parts along dimension 0
- gate_grad: float32 [256, 128, 128], P(('groups', 'fsdp')), parts along dimension 0
- up_grad: float32 [256, 128, 128], P(('groups', 'fsdp')), parts along dimension 0
- down_block_gradient: float32 [256, 128, 128], P(('groups', 'fsdp')), parts along dimension 0
The draws below stay inside these ranges and needn't reach their ends.
There are 2 independent parts, one for each index of `groups`. The reference program is written for one: setup_inputs(seed, part) draws one part's arguments, and reference() takes and returns one part's arrays. A program takes and returns all parts, laid end to end along the dimension named above; an argument that names none is the same for every part. Nothing has to cross between parts.
Inputs may be any that keep to these rules, and one draw needn't show every extreme that they name: `gate_dest`: among the 16 blocks of one projection held by one owner, at most 3 share one offset. `up_dest`: among the 16 blocks of one projection held by one owner, at most 3 share one offset. `down_dest`: among the 16 blocks of one projection held by one owner, at most 3 share one offset.
All inputs are finite; a program needn't handle non-finite values.
Results may differ from the reference program's by a relative error of at most 0.0085.
Values may be sent and summed in bfloat16 or wider, within the bound.
No kernel may reach another device: no remote copies, remote signals or barrier semaphores. Data moves between devices by JAX's collectives and lax.ppermute only.
A program may use at most 64 MiB of HBM per device.

```python
import math
import jax
import jax.numpy as jnp
import numpy as np
from jax import lax

D = 8192
BLK = 128
SLOTS = 16
SPREAD = 8
CAP = 3
TOK_DEV = 128
TOKENS = 256
RB = 64
NB = 128
N_FSDP = 8
N_SECTION = 2


def plant(entries, key, low, high):
    spot = [jax.random.randint(jax.random.fold_in(key, axis), (), 0, length) for axis, length in enumerate(entries.shape)]
    longest = entries.shape.index(max(entries.shape))
    next_to = spot[:longest] + [(spot[longest] + 1) % entries.shape[longest]] + spot[longest + 1:]
    return entries.at[tuple(spot)].set(low).at[tuple(next_to)].set(high)


def steps_of(stream_key, extent, split, smallest, largest):
    def one(dim, blocks):
        draws = jax.random.uniform(jax.random.fold_in(jax.random.fold_in(stream_key, 6), dim), (blocks,), jnp.float32, smallest / len(split), largest / len(split))
        return jnp.repeat(jnp.exp(draws), extent[dim] // blocks).reshape((-1,) + (1,) * (len(extent) - dim - 1))

    factor_of = one(*split[0])
    for cut in split[1:]:
        factor_of = factor_of * one(*cut)
    return factor_of


def assign_block(key, own, number, rows, number_of, top, most, slope):
    ranking = jax.random.permutation(key, number_of)
    heavy_load, ordinary = load_shares(number_of, rows * top, most, slope, True), load_shares(number_of, rows * top, most, slope, False)
    places = jnp.arange(number_of)

    def named(lengths, offset_by):
        used = int((lengths > 0).sum())
        fixed = max(1, used // 4)
        passed = fixed + (places - fixed + offset_by * (used - fixed)) % max(1, number_of - fixed)
        return jnp.zeros((number_of,), jnp.int32).at[ranking[jnp.where(places < fixed, places, passed)]].set(jnp.asarray(lengths, jnp.int32))

    lengths = jnp.where(number % 4 == 0, named(heavy_load, number // 4), named(ordinary, number - number // 4 - 1))
    mixed = jax.random.permutation(jax.random.fold_in(own, 3), number_of)
    donor, taker = mixed[0:number_of // 2 * 2:2], mixed[1:number_of // 2 * 2:2]
    slack = jnp.minimum(lengths[donor] - 1, most - lengths[taker]) // 2
    slack = jnp.where((donor == ranking[0]) | (taker == ranking[0]) | (lengths[taker] == 0), 0, jnp.maximum(slack, 0))
    passed = jax.random.randint(jax.random.fold_in(own, 4), (number_of // 2,), 0, 1 << 20) % (slack + 1)
    lengths = lengths.at[donor].add(-passed).at[taker].add(passed)
    members = jnp.searchsorted(jnp.cumsum(lengths), jnp.arange(rows * top), side="right").astype(jnp.int32)
    table = members.reshape(top, rows).T
    table = table[jax.random.permutation(jax.random.fold_in(own, 1), rows)]
    offset_by = jax.random.randint(jax.random.fold_in(own, 2), (rows, 1), 0, top)
    return jnp.take_along_axis(table, (jnp.arange(top)[None, :] + offset_by) % top, axis=1)


def load_shares(count, total, limit, skew, full):
    loads = [(1 << 20) // math.isqrt(grade ** skew) + 1 for grade in range(1, count + 1)]
    largest = limit if full else min(limit, max(-(-total // count), total * loads[0] // sum(loads)))
    least = 1 if total - largest >= count - 1 else 0
    given, rest = [largest] + [least] * (count - 1), total - largest - least * (count - 1)
    while rest > 0:
        movable = [i for i in range(1, count) if given[i] < largest] or [i for i in range(1, count) if given[i] < limit]
        pool, left = sum([loads[i] for i in movable]), rest
        for i in movable:
            extra = min(limit - given[i], max(1, left * loads[i] // pool), rest)
            given[i] = given[i] + extra
            rest = rest - extra
    return np.array(given)


def scatter_about(key, extent, scale, reach, shards=(), kind=jnp.bfloat16):
    values = scale * jax.random.normal(key, extent, jnp.float32)
    if shards:
        values = values * steps_of(key, extent, shards, -0.22, 0.18)
    return jnp.clip(values, -reach, reach).astype(kind)


def setup_inputs(seed: int = 0, part: int = 0) -> dict:
    keys = jax.random.split(jax.random.key(seed), 12)
    part_splits = jax.random.split(jax.random.fold_in(keys[11], part), 12)
    tokens = scatter_about(part_splits[0], (TOKENS, D), 1.0, 6.0, ((0, 2), (1, 8)))
    cotangent = scatter_about(part_splits[1], (TOKENS, D), 1.0, 6.0, ((0, 2), (1, 8)))
    gate_blocks = scatter_about(keys[2], (NB, BLK, BLK), (SLOTS * BLK) ** -0.5, 0.125, ((0, 8),))
    up_blocks = scatter_about(keys[3], (NB, BLK, BLK), (SLOTS * BLK) ** -0.5, 0.125, ((0, 8),))
    down_blocks = scatter_about(keys[4], (NB, BLK, BLK), (SLOTS * BLK) ** -0.5, 0.125, ((0, 8),))
    gate_dest_keys = jax.random.split(jax.random.fold_in(keys[5], 1), NB // SLOTS)
    gate_dest_turns = jax.random.permutation(jax.random.fold_in(keys[5], 3), NB // SLOTS)
    gate_dest = jax.vmap(lambda own, number: assign_block(jax.random.fold_in(keys[5], 2), own, number, SLOTS, SPREAD, 1, CAP, 2))(gate_dest_keys, gate_dest_turns).reshape((NB, 1))
    up_dest_keys = jax.random.split(jax.random.fold_in(keys[6], 1), NB // SLOTS)
    up_dest_turns = jax.random.permutation(jax.random.fold_in(keys[6], 3), NB // SLOTS)
    up_dest = jax.vmap(lambda own, number: assign_block(jax.random.fold_in(keys[6], 2), own, number, SLOTS, SPREAD, 1, CAP, 2))(up_dest_keys, up_dest_turns).reshape((NB, 1))
    down_dest_keys = jax.random.split(jax.random.fold_in(keys[7], 1), NB // SLOTS)
    down_dest_turns = jax.random.permutation(jax.random.fold_in(keys[7], 3), NB // SLOTS)
    down_dest = jax.vmap(lambda own, number: assign_block(jax.random.fold_in(keys[7], 2), own, number, SLOTS, SPREAD, 1, CAP, 2))(down_dest_keys, down_dest_turns).reshape((NB, 1))
    gate_rows = plant(jax.random.randint(keys[8], (NB,), 0, RB), jax.random.fold_in(keys[8], 1), 0, RB - 1).astype(jnp.int32)
    up_rows = plant(jax.random.randint(keys[9], (NB,), 0, RB), jax.random.fold_in(keys[9], 1), 0, RB - 1).astype(jnp.int32)
    down_rows = plant(jax.random.randint(keys[10], (NB,), 0, RB), jax.random.fold_in(keys[10], 1), 0, RB - 1).astype(jnp.int32)
    return {"tokens": tokens, "cotangent": cotangent, "gate_blocks": gate_blocks, "up_blocks": up_blocks, "down_blocks": down_blocks, "gate_dest": gate_dest, "up_dest": up_dest, "down_dest": down_dest, "gate_rows": gate_rows, "up_rows": up_rows, "down_rows": down_rows}


def columns_of(target):
    owners = jnp.arange(N_FSDP * SLOTS, dtype=jnp.int32) // SLOTS
    return (owners - target[:, 0]) % N_FSDP


def select_rows(field, row_ids):
    grid = field.reshape(field.shape[0], D // BLK, BLK)
    return grid[:, row_ids, :].astype(jnp.float32)


def select_columns(hidden, columns):
    grid = hidden.reshape(hidden.shape[0], N_FSDP, BLK)
    return grid[:, columns, :].astype(jnp.float32)


def collect_columns(terms, columns):
    summed = jax.ops.segment_sum(terms, columns, num_segments=N_FSDP)
    return summed.transpose(1, 0, 2).reshape(terms.shape[1], N_FSDP * BLK)


def collect_rows(terms, row_ids):
    summed = jax.ops.segment_sum(terms, row_ids, num_segments=D // BLK)
    return summed.transpose(1, 0, 2).reshape(terms.shape[1], D)


def section_total(left, right):
    total = jnp.zeros((left.shape[1], BLK, BLK), jnp.float32)
    for section_index in range(N_SECTION):
        lower = section_index * TOK_DEV
        term = jnp.einsum("tjk,tjn->jkn", left[lower:lower + TOK_DEV], right[lower:lower + TOK_DEV])
        total = total + lax.optimization_barrier(term.astype(jnp.bfloat16)).astype(jnp.float32)
    return total


def reference(tokens, cotangent, gate_blocks, up_blocks, down_blocks, gate_dest, up_dest, down_dest, gate_rows, up_rows, down_rows):
    gate_cols = columns_of(gate_dest)
    up_cols = columns_of(up_dest)
    down_cols = columns_of(down_dest)
    gate_w = gate_blocks.astype(jnp.float32)
    up_w = up_blocks.astype(jnp.float32)
    down_w = down_blocks.astype(jnp.float32)
    tok_gate = select_rows(tokens, gate_rows)
    tok_up = select_rows(tokens, up_rows)
    gate = collect_columns(jnp.einsum("tjk,jkn->jtn", tok_gate, gate_w), gate_cols)
    upper = collect_columns(jnp.einsum("tjk,jkn->jtn", tok_up, up_w), up_cols)
    sigma = jax.nn.sigmoid(gate)
    hidden = (gate * sigma * upper).astype(jnp.bfloat16)
    cot_down = select_rows(cotangent, down_rows)
    hidden_grad = collect_columns(jnp.einsum("tjn,jkn->jtk", cot_down, down_w), down_cols)
    gate_d = (hidden_grad * upper * sigma * (1.0 + gate * (1.0 - sigma))).astype(jnp.bfloat16)
    up_d = (hidden_grad * gate * sigma).astype(jnp.bfloat16)
    gate_d_sel = select_columns(gate_d, gate_cols)
    up_d_sel = select_columns(up_d, up_cols)
    gate_grad = section_total(tok_gate, gate_d_sel)
    up_grad = section_total(tok_up, up_d_sel)
    down_block_gradient = section_total(select_columns(hidden, down_cols), cot_down)
    input_grad = collect_rows(jnp.einsum("tjn,jkn->jtk", gate_d_sel, gate_w), gate_rows)
    input_grad = input_grad + collect_rows(jnp.einsum("tjn,jkn->jtk", up_d_sel, up_w), up_rows)
    return input_grad.astype(jnp.bfloat16), gate_grad, up_grad, down_block_gradient
```

```python
import functools

import jax
import jax.numpy as jnp
from jax import lax
from jax.experimental import pallas as pl
from jax.experimental.pallas import tpu as pltpu
from jax.sharding import PartitionSpec as P

BLK = 128
SPREAD = 8
CAP = 3
KINDS = 3
PER = KINDS * CAP
VMEM_LIMIT = 56 * 1024 * 1024

F32 = jnp.float32
BF16 = jnp.bfloat16
ANY = pl.BlockSpec(memory_space=pl.ANY)
VMEM = pl.BlockSpec(memory_space=pltpu.VMEM)
SMEM = pl.BlockSpec(memory_space=pltpu.SMEM)


def params():
    return pltpu.CompilerParams(vmem_limit_bytes=VMEM_LIMIT)


def shape(dims, dtype=BF16):
    return jax.ShapeDtypeStruct(dims, dtype)


def ring_order(count):
    return [*range(0, count, 2), *range(count - 1, 0, -2)]


def ring_routes(count):
    order = ring_order(count)
    onward = [(order[i], order[(i + 1) % count]) for i in range(count)]
    return onward, [(b, a) for a, b in onward]


def shift(block, axis, distance):
    count = lax.axis_size(axis)
    return lax.ppermute(block, axis, [(i, (i + distance) % count) for i in range(count)])


def swap(block, axis):
    return lax.ppermute(block, axis, [(0, 1), (1, 0)])


def ring_gather(block, axis):
    count = lax.axis_size(axis)
    onward, back = ring_routes(count)
    order = ring_order(count)
    place = jnp.array([order.index(i) for i in range(count)], jnp.int32)[lax.axis_index(axis)]
    table = jnp.array(order, jnp.int32)
    half = block.shape[0] // 2
    pieces = [(block, lax.axis_index(axis), 0)]
    left = right = block
    for step in range(1, count // 2):
        left = lax.ppermute(left, axis, onward)
        right = lax.ppermute(right, axis, back)
        pieces.append((left, table[(place - step) % count], 0))
        pieces.append((right, table[(place + step) % count], 0))
    far = table[(place + count // 2) % count]
    pieces.append((lax.ppermute(left[:half], axis, onward), far, 0))
    pieces.append((lax.ppermute(right[half:], axis, back), far, half))
    return pieces


def pack_kernel(info, gd, ud, dd, gr, ur, dr, gate, up, down, *refs):
    own = refs[0]
    sends = refs[1:SPREAD]
    slab, ids, used = refs[SPREAD:]
    quarter = info[0]
    rows = BLK // 4
    slab[...] = jnp.zeros_like(slab)
    own[...] = jnp.zeros_like(own)
    ids[...] = jnp.zeros_like(ids)
    for kind, (dest, row_ids, blocks) in enumerate(((gd, gr, gate), (ud, ur, up), (dd, dr, down))):
        for offset in range(SPREAD):
            used[offset] = 0

        def place(j, carry, kind=kind, dest=dest, row_ids=row_ids, blocks=blocks):
            offset = dest[j]
            rank = used[offset]
            used[offset] = rank + 1
            slot = kind * CAP + rank
            start = pl.multiple_of(quarter * rows, rows)
            slab[offset, slot] = blocks[j, pl.ds(start, rows), :]
            ids[offset, pl.ds(slot, 1), :] = jnp.full((1, BLK), row_ids[j].astype(F32), F32)

            @pl.when(offset == 0)
            def _():
                own[slot] = blocks[j]

            return carry

        lax.fori_loop(0, blocks.shape[0], place, 0)
    for offset in range(1, SPREAD):
        sends[offset - 1][0:PER] = slab[offset]
        sends[offset - 1][PER] = ids[offset].astype(BF16)
    own[PER, 0:rows] = ids[0].astype(BF16)


def pack(quarter, dests, row_ids, blocks):
    rows = BLK // 4
    return pl.pallas_call(
        pack_kernel,
        out_shape=[shape((PER + 1, BLK, BLK))] + [shape((PER + 1, rows, BLK))] * (SPREAD - 1),
        in_specs=[SMEM] * 7 + [VMEM] * 3,
        out_specs=[VMEM] * SPREAD,
        scratch_shapes=[
            pltpu.VMEM((SPREAD, PER, rows, BLK), BF16),
            pltpu.VMEM((SPREAD, rows, BLK), F32),
            pltpu.SMEM((SPREAD,), jnp.int32),
        ],
        compiler_params=params(),
        name="pack",
    )(quarter, *dests, *row_ids, *blocks)


def forward_kernel(layout, tokens_here, split, info, own, w0, w1, w2, w3, *refs):
    count = len(layout)
    shards = refs[:count]
    refs = refs[count:]
    field_out, hidden_out = refs[0], refs[1]
    outs = refs[2 : 3 + 3 * split]
    field, weights, id_rows, id_ints, id_scalars, left, total, shard_sems, sems = refs[3 + 3 * split :]
    width = field.shape[2]
    per_piece = width // BLK
    t = tokens_here

    own_copies = [
        pltpu.make_async_copy(own.at[0:PER], weights.at[0], sems.at[0]),
        pltpu.make_async_copy(own.at[PER, 0 : BLK // 4], id_rows.at[0], sems.at[1]),
        pltpu.make_async_copy(w0.at[:, PER], id_rows.at[1:SPREAD], sems.at[2]),
    ]
    weight_copies = []
    for n, ref in enumerate((w0, w1, w2, w3)):
        begin = pl.multiple_of(info[1 + n] * (BLK // 4), BLK // 4)
        weight_copies.append(
            pltpu.make_async_copy(
                ref.at[:, 0:PER],
                weights.at[1:SPREAD, :, pl.ds(begin, BLK // 4), :],
                sems.at[3 + n],
            )
        )
    shard_copies = []
    for n, (first, length) in enumerate(layout):
        shard_copies.append(
            pltpu.make_async_copy(
                shards[n], field.at[info[5 + n], first : first + length], shard_sems.at[n]
            )
        )
    for copy in own_copies + shard_copies + weight_copies:
        copy.start()
    total[...] = jnp.zeros_like(total)
    for copy in own_copies[1:]:
        copy.wait()
    id_ints[...] = id_rows[:, 0:16, :].astype(F32).astype(jnp.int32)
    id_copy = pltpu.make_async_copy(id_ints, id_scalars, sems.at[7])
    id_copy.start()
    for copy in shard_copies:
        copy.wait()
    field_copy = pltpu.make_async_copy(field, field_out, sems.at[8])
    field_copy.start()
    id_copy.wait()

    def where(offset, kind, rank):
        row = id_scalars[offset, kind * CAP + rank, 0]
        return row // per_piece, pl.multiple_of((row % per_piece) * BLK, BLK)

    for kind in range(KINDS):
        first = t if kind == 2 else 0
        for offset in range(SPREAD):
            for rank in range(CAP):
                piece, column = where(offset, kind, rank)
                n = offset * CAP + rank
                left[kind, :, n * BLK : (n + 1) * BLK] = field[
                    piece, first : first + t, pl.ds(column, BLK)
                ]
    own_copies[0].wait()
    for copy in weight_copies:
        copy.wait()

    def block_group(kind):
        return weights[:, kind * CAP : (kind + 1) * CAP].reshape(SPREAD * CAP * BLK, BLK)

    gate = jnp.dot(left[0], block_group(0), preferred_element_type=F32)
    upper = jnp.dot(left[1], block_group(1), preferred_element_type=F32)
    nt = (((1,), (1,)), ((), ()))
    hidden_grad = jnp.zeros((t, BLK), F32)
    for offset in range(SPREAD):
        for rank in range(CAP):
            n = offset * CAP + rank
            hidden_grad = hidden_grad + lax.dot_general(
                left[2, :, n * BLK : (n + 1) * BLK],
                weights[offset, 2 * CAP + rank],
                nt,
                preferred_element_type=F32,
            )
    sigma = 1.0 / (1.0 + jnp.exp(-gate))
    hidden = (gate * sigma * upper).astype(BF16)
    gate_d = (hidden_grad * upper * sigma * (1.0 + gate * (1.0 - sigma))).astype(BF16)
    up_d = (hidden_grad * gate * sigma).astype(BF16)
    hidden_out[0] = gate_d
    hidden_out[1] = up_d
    hidden_out[2] = hidden
    for kind, grad in ((0, gate_d), (1, up_d)):
        for offset in range(SPREAD):
            terms = lax.dot_general(
                grad,
                weights[offset, kind * CAP : (kind + 1) * CAP].reshape(CAP * BLK, BLK),
                nt,
                preferred_element_type=F32,
            )
            for rank in range(CAP):
                piece, column = where(offset, kind, rank)
                total[piece, :, pl.ds(column, BLK)] += terms[:, rank * BLK : (rank + 1) * BLK]
    if split:
        side = info[0]
        send_a, send_b, keep_a, keep_b = outs
        h = t // 2
        for z in range(send_a.shape[0]):
            away = total[2 * z + 1 - side].astype(BF16)
            here = total[2 * z + side].astype(BF16)
            send_a[z] = away[:h]
            send_b[z] = away[h:]
            keep_a[z] = here[:h]
            keep_b[z] = here[h:]
    else:
        outs[0][...] = total[...].astype(BF16)
    field_copy.wait()


def forward(info, own, quarters, pieces, split, piece_count):
    layout = [(first, block.shape[0]) for block, _, first in pieces]
    t = pieces[0][0].shape[0] // 2
    width = pieces[0][0].shape[1]
    if split:
        outs = [shape((piece_count // 2, t // 2, width))] * 4
    else:
        outs = [shape((piece_count, t, width))]
    field = (piece_count, 2 * t, width)
    return pl.pallas_call(
        functools.partial(forward_kernel, layout, t, int(split)),
        out_shape=[shape(field), shape((KINDS, t, BLK))] + outs,
        in_specs=[SMEM] + [ANY] * (5 + len(pieces)),
        out_specs=[ANY] + [VMEM] * (1 + len(outs)),
        scratch_shapes=[
            pltpu.VMEM(field, BF16),
            pltpu.VMEM((SPREAD, PER, BLK, BLK), BF16),
            pltpu.VMEM((SPREAD, BLK // 4, BLK), BF16),
            pltpu.VMEM((SPREAD, 16, BLK), jnp.int32),
            pltpu.SMEM((SPREAD, 16, BLK), jnp.int32),
            pltpu.VMEM((KINDS, t, SPREAD * CAP * BLK), BF16),
            pltpu.VMEM((piece_count, t, width), F32),
            pltpu.SemaphoreType.DMA((len(pieces),)),
            pltpu.SemaphoreType.DMA((9,)),
        ],
        compiler_params=params(),
        name="forward",
    )(info, own, *quarters, *[block for block, _, _ in pieces])


def pair_kernel(info, keep, got, here, one, two, three):
    z = info[0]
    for step, ref in enumerate((here, one, two, three)):
        at = lax.rem(z + step, keep.shape[0])
        ref[...] = (keep[at].astype(F32) + got[at].astype(F32)).astype(BF16)


def pair(z, keep, got):
    piece = shape(keep.shape[1:])
    return pl.pallas_call(
        pair_kernel,
        out_shape=[piece] * 4,
        in_specs=[SMEM, VMEM, VMEM],
        out_specs=[VMEM] * 4,
        compiler_params=params(),
        name="pair",
    )(z, keep, got)


def grads_kernel(layout, info, gd, ud, dd, gr, ur, dr, field, *refs):
    count = len(layout)
    arrived = refs[:count]
    out, columns, sems = refs[count:]
    t = field.shape[1] // 2
    per_piece = field.shape[2] // BLK
    copies = []
    for n, (first, length) in enumerate(layout):
        copies.append(
            pltpu.make_async_copy(
                arrived[n], columns.at[info[n], first : first + length], sems.at[n]
            )
        )
    for copy in copies:
        copy.start()
    for copy in copies:
        copy.wait()
    tn = (((0,), (0,)), ((), ()))
    slots = gd.shape[0]
    for kind, (dest, row_ids) in enumerate(((gd, gr), (ud, ur), (dd, dr))):
        first = t if kind == 2 else 0

        def one(j, carry, kind=kind, dest=dest, row_ids=row_ids, first=first):
            row = row_ids[j]
            column = pl.multiple_of((row % per_piece) * BLK, BLK)
            part = field[row // per_piece, first : first + t, pl.ds(column, BLK)]
            side = columns[dest[j], kind * t : (kind + 1) * t, :]
            pair_of = (side, part) if kind == 2 else (part, side)
            out[kind * slots + j] = lax.dot_general(
                *pair_of, tn, preferred_element_type=F32
            ).astype(BF16)
            return carry

        lax.fori_loop(0, slots, one, 0, unroll=4)


def grads(info, dests, row_ids, field, pieces):
    layout = [(first, block.shape[0]) for block, _, first in pieces]
    rows = pieces[0][0].shape[0]
    slots = dests[0].shape[0]
    return pl.pallas_call(
        functools.partial(grads_kernel, layout),
        out_shape=shape((KINDS * slots, BLK, BLK)),
        in_specs=[SMEM] * 7 + [VMEM] + [ANY] * len(pieces),
        out_specs=VMEM,
        scratch_shapes=[
            pltpu.VMEM((SPREAD, rows, BLK), BF16),
            pltpu.SemaphoreType.DMA((len(pieces),)),
        ],
        compiler_params=params(),
        name="grads",
    )(info, *dests, *row_ids, field, *[block for block, _, _ in pieces])


def shards(
    tokens,
    cotangent,
    gate_blocks,
    up_blocks,
    down_blocks,
    gate_dest,
    up_dest,
    down_dest,
    gate_rows,
    up_rows,
    down_rows,
):
    count = lax.axis_size("fsdp")
    me = lax.axis_index("fsdp")
    group = lax.axis_index("groups")
    section = lax.axis_index("section")
    grid = count == SPREAD and tokens.shape[1] % BLK == 0
    t = tokens.shape[0]
    dests = [target[:, 0] for target in (gate_dest, up_dest, down_dest)]
    row_ids = [gate_rows, up_rows, down_rows]

    both = jnp.concatenate([tokens, cotangent], axis=0)
    if grid:
        pieces = ring_gather(both, "fsdp")
        piece_count = count
    else:
        pieces = [(lax.all_gather(both, "fsdp", axis=1, tiled=True), jnp.int32(0), 0)]
        piece_count = 1

    quarter = jnp.reshape(2 * group + section, (1,)).astype(jnp.int32)
    own, *sends = pack(quarter, dests, row_ids, (gate_blocks, up_blocks, down_blocks))
    mine = jnp.stack([shift(block, "fsdp", -d) for d, block in enumerate(sends, 1)], axis=0)
    across = swap(mine, "groups")
    beside = swap(mine, "section")
    diagonal = swap(across, "section")
    quarters = (mine, beside, across, diagonal)
    order_of_quarters = [
        2 * group + section,
        2 * group + 1 - section,
        2 * (1 - group) + section,
        2 * (1 - group) + 1 - section,
    ]
    info = jnp.stack(
        [me % 2, *order_of_quarters, *[source for _, source, _ in pieces]]
    ).astype(jnp.int32)
    field, columns, *partial_input = forward(info, own, quarters, pieces, grid, piece_count)

    flat = columns.reshape(KINDS * t, BLK)
    if grid:
        arrived = [
            (block, (me - source) % count, first)
            for block, source, first in ring_gather(flat, "fsdp")
        ]
    else:
        arrived = [(flat, jnp.int32(0), 0)] + [
            (shift(flat, "fsdp", d), jnp.int32(d), 0) for d in range(1, SPREAD)
        ]
    offsets = jnp.stack([offset for _, offset, _ in arrived]).astype(jnp.int32)
    part = grads(offsets, dests, row_ids, field, arrived)
    other = swap(part, "section")
    summed = part.astype(F32) + other.astype(F32)
    slots = gate_blocks.shape[0]
    gate_grad, up_grad, down_grad = (
        summed[kind * slots : (kind + 1) * slots] for kind in range(KINDS)
    )

    if grid:
        beside_x = [(i, i ^ 1) for i in range(count)]
        along_z = [
            [(i, (i + 2 * step) % count) for i in range(count)] for step in range(1, count // 2)
        ]
        z = jnp.reshape(me // 2, (1,)).astype(jnp.int32)
        send_a, send_b, keep_a, keep_b = partial_input
        halves = []
        for send, keep in ((send_a, keep_a), (send_b, keep_b)):
            got = lax.ppermute(send, "fsdp", beside_x)
            here, *away = pair(z, keep, got)
            result = here.astype(F32)
            for block, route in zip(away, along_z, strict=True):
                result = result + lax.ppermute(block, "fsdp", route).astype(F32)
            halves.append(result.astype(BF16))
        input_grad = jnp.concatenate(halves, axis=0)
    else:
        input_grad = lax.psum_scatter(
            partial_input[0].reshape(t, -1), "fsdp", scatter_dimension=1, tiled=True
        )
    return input_grad, gate_grad, up_grad, down_grad


def solution(mesh):
    return jax.shard_map(
        shards,
        mesh=mesh,
        in_specs=(
            P(("groups", "section"), "fsdp"),
            P(("groups", "section"), "fsdp"),
            P("fsdp", None, None),
            P("fsdp", None, None),
            P("fsdp", None, None),
            P("fsdp", None),
            P("fsdp", None),
            P("fsdp", None),
            P("fsdp"),
            P("fsdp"),
            P("fsdp"),
        ),
        out_specs=(
            P(("groups", "section"), "fsdp"),
            P(("groups", "fsdp"), None, None),
            P(("groups", "fsdp"), None, None),
            P(("groups", "fsdp"), None, None),
        ),
        check_vma=False,
    )
```

```python
import functools

import jax
import jax.numpy as jnp
from jax import lax
from jax.experimental import pallas as pl
from jax.experimental.pallas import tpu as pltpu
from jax.sharding import PartitionSpec as P

BLK = 128
SPREAD = 8
CAP = 3
KINDS = 3
PER = KINDS * CAP
VMEM_LIMIT = 56 * 1024 * 1024

F32 = jnp.float32
BF16 = jnp.bfloat16
ANY = pl.BlockSpec(memory_space=pl.ANY)
VMEM = pl.BlockSpec(memory_space=pltpu.VMEM)
SMEM = pl.BlockSpec(memory_space=pltpu.SMEM)


def params():
    return pltpu.CompilerParams(vmem_limit_bytes=VMEM_LIMIT)


def shape(dims, dtype=BF16):
    return jax.ShapeDtypeStruct(dims, dtype)


def ring_at(place, count):
    place = place % count
    return jnp.where(place < count // 2, 2 * place, 2 * (count - 1 - place) + 1)


def ring_place(index, count):
    return jnp.where(index % 2 == 0, index // 2, count - 1 - index // 2)


def ring_routes(count):
    order = [*range(0, count, 2), *range(count - 1, 0, -2)]
    onward = [(order[i], order[(i + 1) % count]) for i in range(count)]
    return onward, [(b, a) for a, b in onward]


def shift(block, axis, distance):
    count = lax.axis_size(axis)
    return lax.ppermute(block, axis, [(i, (i + distance) % count) for i in range(count)])


def swap(block, axis):
    return lax.ppermute(block, axis, [(0, 1), (1, 0)])


def tie(block, *others):
    return lax.optimization_barrier((block, *others))[0]


def ring_gather(block, axis, hold=None):
    count = lax.axis_size(axis)
    onward, back = ring_routes(count)
    half = block.shape[0] // 2
    pieces = [(block, 0, 0)]
    left = right = block
    for step in range(1, count // 2):
        if hold is not None and step == hold[0]:
            left, right, _ = lax.optimization_barrier((left, right, hold[1]))
        left = lax.ppermute(left, axis, onward)
        right = lax.ppermute(right, axis, back)
        pieces.append((left, -step, 0))
        pieces.append((right, step, 0))
    pieces.append((lax.ppermute(left[:half], axis, onward), count // 2, 0))
    pieces.append((lax.ppermute(right[half:], axis, back), count // 2, half))
    return pieces


def pack_kernel(gd, ud, dd, gr, ur, dr, tokens, cotangent, gate, up, down, *refs):
    both, own = refs[:2]
    sends = refs[2 : SPREAD + 1]
    slab, ids, used = refs[SPREAD + 1 :]
    quarter = 2 * lax.axis_index("groups") + lax.axis_index("section")
    t = tokens.shape[0]
    both[0:t] = tokens[...]
    both[t : 2 * t] = cotangent[...]
    rows = BLK // 4
    slab[...] = jnp.zeros_like(slab)
    own[...] = jnp.zeros_like(own)
    ids[...] = jnp.zeros_like(ids)
    for kind, (dest, row_ids, blocks) in enumerate(((gd, gr, gate), (ud, ur, up), (dd, dr, down))):
        for offset in range(SPREAD):
            used[offset] = 0

        def place(j, carry, kind=kind, dest=dest, row_ids=row_ids, blocks=blocks):
            offset = dest[j]
            rank = used[offset]
            used[offset] = rank + 1
            slot = kind * CAP + rank
            start = pl.multiple_of(quarter * rows, rows)
            slab[offset, slot] = blocks[j, pl.ds(start, rows), :]
            ids[offset, pl.ds(slot, 1), :] = jnp.full((1, BLK), row_ids[j].astype(F32), F32)

            @pl.when(offset == 0)
            def _():
                own[slot] = blocks[j]

            return carry

        lax.fori_loop(0, blocks.shape[0], place, 0)
    for offset in range(1, SPREAD):
        sends[offset - 1][0:PER] = slab[offset]
        sends[offset - 1][PER] = ids[offset].astype(BF16)
    own[PER, 0:rows] = ids[0].astype(BF16)


def pack(tokens, cotangent, dests, row_ids, blocks):
    rows = BLK // 4
    t, width = tokens.shape
    return pl.pallas_call(
        pack_kernel,
        out_shape=[shape((2 * t, width)), shape((PER + 1, BLK, BLK))]
        + [shape((PER + 1, rows, BLK))] * (SPREAD - 1),
        in_specs=[SMEM] * 6 + [VMEM] * 5,
        out_specs=[VMEM] * (SPREAD + 1),
        scratch_shapes=[
            pltpu.VMEM((SPREAD, PER, rows, BLK), BF16),
            pltpu.VMEM((SPREAD, rows, BLK), F32),
            pltpu.SMEM((SPREAD,), jnp.int32),
        ],
        compiler_params=params(),
        name="pack",
    )(*dests, *row_ids, tokens, cotangent, *blocks)


def forward_kernel(layout, tokens_here, split, own, w0, w1, w2, w3, *refs):
    count = len(layout)
    shards = refs[:count]
    refs = refs[count:]
    field_out, hidden_out = refs[0], refs[1]
    outs = refs[2 : 3 + 3 * split]
    field, weights, id_rows, id_ints, id_scalars, left, total, shard_sems, sems = refs[3 + 3 * split :]
    width = field.shape[2]
    per_piece = width // BLK
    t = tokens_here
    axis_size = lax.axis_size("fsdp")
    me = lax.axis_index("fsdp")
    group = lax.axis_index("groups")
    section = lax.axis_index("section")
    quarters = (
        2 * group + section,
        2 * group + 1 - section,
        2 * (1 - group) + section,
        2 * (1 - group) + 1 - section,
    )

    own_copies = [
        pltpu.make_async_copy(own.at[0:PER], weights.at[0], sems.at[0]),
        pltpu.make_async_copy(own.at[PER, 0 : BLK // 4], id_rows.at[0], sems.at[1]),
        pltpu.make_async_copy(w0.at[:, PER], id_rows.at[1:SPREAD], sems.at[2]),
    ]
    weight_copies = []
    for n, ref in enumerate((w0, w1, w2, w3)):
        begin = pl.multiple_of(quarters[n] * (BLK // 4), BLK // 4)
        weight_copies.append(
            pltpu.make_async_copy(
                ref.at[:, 0:PER],
                weights.at[1:SPREAD, :, pl.ds(begin, BLK // 4), :],
                sems.at[3 + n],
            )
        )
    shard_copies = []
    for n, (steps, first, length) in enumerate(layout):
        piece = ring_at(ring_place(me, axis_size) + steps, axis_size) if split else 0
        shard_copies.append(
            pltpu.make_async_copy(
                shards[n], field.at[piece, first : first + length], shard_sems.at[n]
            )
        )
    for copy in own_copies + shard_copies + weight_copies:
        copy.start()
    total[...] = jnp.zeros_like(total)
    for copy in own_copies[1:]:
        copy.wait()
    id_ints[...] = id_rows[:, 0:16, :].astype(F32).astype(jnp.int32)
    id_copy = pltpu.make_async_copy(id_ints, id_scalars, sems.at[7])
    id_copy.start()
    for copy in shard_copies:
        copy.wait()
    field_copy = pltpu.make_async_copy(field, field_out, sems.at[8])
    field_copy.start()
    id_copy.wait()

    def where(offset, kind, rank):
        row = id_scalars[offset, kind * CAP + rank, 0]
        return row // per_piece, pl.multiple_of((row % per_piece) * BLK, BLK)

    for kind in range(KINDS):
        first = t if kind == 2 else 0
        for offset in range(SPREAD):
            for rank in range(CAP):
                piece, column = where(offset, kind, rank)
                n = offset * CAP + rank
                left[kind, :, n * BLK : (n + 1) * BLK] = field[
                    piece, first : first + t, pl.ds(column, BLK)
                ]
    own_copies[0].wait()
    for copy in weight_copies:
        copy.wait()

    def block_group(kind):
        return weights[:, kind * CAP : (kind + 1) * CAP].reshape(SPREAD * CAP * BLK, BLK)

    gate = jnp.dot(left[0], block_group(0), preferred_element_type=F32)
    upper = jnp.dot(left[1], block_group(1), preferred_element_type=F32)
    nt = (((1,), (1,)), ((), ()))
    hidden_grad = jnp.zeros((t, BLK), F32)
    for offset in range(SPREAD):
        for rank in range(CAP):
            n = offset * CAP + rank
            hidden_grad = hidden_grad + lax.dot_general(
                left[2, :, n * BLK : (n + 1) * BLK],
                weights[offset, 2 * CAP + rank],
                nt,
                preferred_element_type=F32,
            )
    sigma = 1.0 / (1.0 + jnp.exp(-gate))
    hidden = (gate * sigma * upper).astype(BF16)
    gate_d = (hidden_grad * upper * sigma * (1.0 + gate * (1.0 - sigma))).astype(BF16)
    up_d = (hidden_grad * gate * sigma).astype(BF16)
    hidden_out[0] = gate_d
    hidden_out[1] = up_d
    hidden_out[2] = hidden
    for kind, grad in ((0, gate_d), (1, up_d)):
        for offset in range(SPREAD):
            terms = lax.dot_general(
                grad,
                weights[offset, kind * CAP : (kind + 1) * CAP].reshape(CAP * BLK, BLK),
                nt,
                preferred_element_type=F32,
            )
            for rank in range(CAP):
                piece, column = where(offset, kind, rank)
                total[piece, :, pl.ds(column, BLK)] += terms[:, rank * BLK : (rank + 1) * BLK]
    if split:
        side = me % 2
        send_a, send_b, keep_a, keep_b = outs
        h = t // 2
        for z in range(send_a.shape[0]):
            away = total[2 * z + 1 - side].astype(BF16)
            here = total[2 * z + side].astype(BF16)
            send_a[z] = away[:h]
            send_b[z] = away[h:]
            keep_a[z] = here[:h]
            keep_b[z] = here[h:]
    else:
        outs[0][...] = total[...].astype(BF16)
    field_copy.wait()


def forward(own, quarters, pieces, split, piece_count):
    layout = [(steps, first, block.shape[0]) for block, steps, first in pieces]
    t = pieces[0][0].shape[0] // 2
    width = pieces[0][0].shape[1]
    if split:
        outs = [shape((piece_count // 2, t // 2, width))] * 4
    else:
        outs = [shape((piece_count, t, width))]
    field = (piece_count, 2 * t, width)
    return pl.pallas_call(
        functools.partial(forward_kernel, layout, t, int(split)),
        out_shape=[shape(field), shape((KINDS, t, BLK))] + outs,
        in_specs=[ANY] * (5 + len(pieces)),
        out_specs=[ANY] + [VMEM] * (1 + len(outs)),
        scratch_shapes=[
            pltpu.VMEM(field, BF16),
            pltpu.VMEM((SPREAD, PER, BLK, BLK), BF16),
            pltpu.VMEM((SPREAD, BLK // 4, BLK), BF16),
            pltpu.VMEM((SPREAD, 16, BLK), jnp.int32),
            pltpu.SMEM((SPREAD, 16, BLK), jnp.int32),
            pltpu.VMEM((KINDS, t, SPREAD * CAP * BLK), BF16),
            pltpu.VMEM((piece_count, t, width), F32),
            pltpu.SemaphoreType.DMA((len(pieces),)),
            pltpu.SemaphoreType.DMA((9,)),
        ],
        compiler_params=params(),
        name="forward",
    )(own, *quarters, *[block for block, _, _ in pieces])


def pair_kernel(keep, got, here, one, two, three):
    z = lax.axis_index("fsdp") // 2
    for step, ref in enumerate((here, one, two, three)):
        at = lax.rem(z + step, keep.shape[0])
        ref[...] = (keep[at].astype(F32) + got[at].astype(F32)).astype(BF16)


def pair(keep, got):
    piece = shape(keep.shape[1:])
    return pl.pallas_call(
        pair_kernel,
        out_shape=[piece] * 4,
        in_specs=[VMEM, VMEM],
        out_specs=[VMEM] * 4,
        compiler_params=params(),
        name="pair",
    )(keep, got)


def grads_kernel(layout, grid, gd, ud, dd, gr, ur, dr, field, *refs):
    count = len(layout)
    arrived = refs[:count]
    out, columns, sems = refs[-3:]
    axis_size = lax.axis_size("fsdp")
    me = lax.axis_index("fsdp")
    t = field.shape[1] // 2
    per_piece = field.shape[2] // BLK
    copies = []
    for n, (steps, first, length) in enumerate(layout):
        offset = steps
        if grid:
            source = ring_at(ring_place(me, axis_size) + steps, axis_size)
            offset = (me - source + axis_size) % axis_size
        copies.append(
            pltpu.make_async_copy(
                arrived[n], columns.at[offset, first : first + length], sems.at[n]
            )
        )
    for copy in copies:
        copy.start()
    for copy in copies:
        copy.wait()
    tn = (((0,), (0,)), ((), ()))
    slots = gd.shape[0]
    for kind, (dest, row_ids) in enumerate(((gd, gr), (ud, ur), (dd, dr))):
        first = t if kind == 2 else 0

        def one(j, carry, kind=kind, dest=dest, row_ids=row_ids, first=first):
            row = row_ids[j]
            column = pl.multiple_of((row % per_piece) * BLK, BLK)
            part = field[row // per_piece, first : first + t, pl.ds(column, BLK)]
            side = columns[dest[j], kind * t : (kind + 1) * t, :]
            pair_of = (side, part) if kind == 2 else (part, side)
            out[kind * slots + j] = lax.dot_general(
                *pair_of, tn, preferred_element_type=F32
            ).astype(BF16)
            return carry

        lax.fori_loop(0, slots, one, 0, unroll=4)


def grads(dests, row_ids, field, pieces, grid, after):
    layout = [(steps, first, block.shape[0]) for block, steps, first in pieces]
    rows = pieces[0][0].shape[0]
    slots = dests[0].shape[0]
    return pl.pallas_call(
        functools.partial(grads_kernel, layout, grid),
        out_shape=shape((KINDS * slots, BLK, BLK)),
        in_specs=[SMEM] * 6 + [VMEM] + [ANY] * (len(pieces) + len(after)),
        out_specs=VMEM,
        scratch_shapes=[
            pltpu.VMEM((SPREAD, rows, BLK), BF16),
            pltpu.SemaphoreType.DMA((len(pieces),)),
        ],
        compiler_params=params(),
        name="grads",
    )(*dests, *row_ids, field, *[block for block, _, _ in pieces], *after)


def shards(
    tokens,
    cotangent,
    gate_blocks,
    up_blocks,
    down_blocks,
    gate_dest,
    up_dest,
    down_dest,
    gate_rows,
    up_rows,
    down_rows,
):
    count = lax.axis_size("fsdp")
    grid = count == SPREAD and tokens.shape[1] % BLK == 0
    t = tokens.shape[0]
    dests = [target[:, 0] for target in (gate_dest, up_dest, down_dest)]
    row_ids = [gate_rows, up_rows, down_rows]

    both, own, *sends = pack(
        tokens, cotangent, dests, row_ids, (gate_blocks, up_blocks, down_blocks)
    )
    if grid:
        pieces = ring_gather(both, "fsdp")
        piece_count = count
    else:
        pieces = [(lax.all_gather(both, "fsdp", axis=1, tiled=True), 0, 0)]
        piece_count = 1

    mine = jnp.stack([shift(block, "fsdp", -d) for d, block in enumerate(sends, 1)], axis=0)
    across = swap(mine, "groups")
    beside = swap(mine, "section")
    diagonal = swap(across, "section")
    quarters = (mine, beside, across, diagonal)
    field, columns, *partial_input = forward(own, quarters, pieces, grid, piece_count)
    flat = columns.reshape(KINDS * t, BLK)

    if grid:
        beside_x = [(i, i ^ 1) for i in range(count)]
        along_z = [
            [(i, (i + 2 * step) % count) for i in range(count)] for step in range(1, count // 2)
        ]
        send_a, send_b, keep_a, keep_b = partial_input
        got_a = lax.ppermute(send_a, "fsdp", beside_x)
        got_b = lax.ppermute(send_b, "fsdp", beside_x)
        halves = []
        for keep, got in ((keep_a, got_a), (keep_b, got_b)):
            here, *away = pair(keep, got)
            halves.append((here, [(b, r) for b, r in zip(away, along_z, strict=True)]))
        sums = []
        for here, away in halves:
            result = here.astype(F32)
            for block, route in away:
                result = result + lax.ppermute(block, "fsdp", route).astype(F32)
            sums.append(result.astype(BF16))
        input_grad = jnp.concatenate(sums, axis=0)
    else:
        input_grad = lax.psum_scatter(
            partial_input[0].reshape(t, -1), "fsdp", scatter_dimension=1, tiled=True
        )

    if grid:
        arrived = ring_gather(flat, "fsdp", (3, halves[0][0]))
        after = [got_b]
    else:
        arrived = [(flat, 0, 0)] + [(shift(flat, "fsdp", d), d, 0) for d in range(1, SPREAD)]
        after = []
    part = grads(dests, row_ids, field, arrived, grid, after)
    other = swap(part, "section")
    summed = part.astype(F32) + other.astype(F32)
    slots = gate_blocks.shape[0]
    gate_grad, up_grad, down_grad = (
        summed[kind * slots : (kind + 1) * slots] for kind in range(KINDS)
    )
    return input_grad, gate_grad, up_grad, down_grad


def solution(mesh):
    return jax.shard_map(
        shards,
        mesh=mesh,
        in_specs=(
            P(("groups", "section"), "fsdp"),
            P(("groups", "section"), "fsdp"),
            P("fsdp", None, None),
            P("fsdp", None, None),
            P("fsdp", None, None),
            P("fsdp", None),
            P("fsdp", None),
            P("fsdp", None),
            P("fsdp"),
            P("fsdp"),
            P("fsdp"),
        ),
        out_specs=(
            P(("groups", "section"), "fsdp"),
            P(("groups", "fsdp"), None, None),
            P(("groups", "fsdp"), None, None),
            P(("groups", "fsdp"), None, None),
        ),
        check_vma=False,
    )
```

```python
import functools

import jax
import jax.numpy as jnp
from jax import lax
from jax.experimental import pallas as pl
from jax.experimental.pallas import tpu as pltpu
from jax.sharding import PartitionSpec as P

BLK = 128
SPREAD = 8
CAP = 3
KINDS = 3
PER = KINDS * CAP
VMEM_LIMIT = 56 * 1024 * 1024

F32 = jnp.float32
BF16 = jnp.bfloat16
ANY = pl.BlockSpec(memory_space=pl.ANY)
VMEM = pl.BlockSpec(memory_space=pltpu.VMEM)
SMEM = pl.BlockSpec(memory_space=pltpu.SMEM)


def params():
    return pltpu.CompilerParams(vmem_limit_bytes=VMEM_LIMIT)


def cost(micros):
    return pl.CostEstimate(flops=0, bytes_accessed=int(micros * 3.5e6), transcendentals=0)


def shape(dims, dtype=BF16):
    return jax.ShapeDtypeStruct(dims, dtype)


def ring_at(place, count):
    place = place % count
    return jnp.where(place < count // 2, 2 * place, 2 * (count - 1 - place) + 1)


def ring_place(index, count):
    return jnp.where(index % 2 == 0, index // 2, count - 1 - index // 2)


def ring_routes(count):
    order = [*range(0, count, 2), *range(count - 1, 0, -2)]
    onward = [(order[i], order[(i + 1) % count]) for i in range(count)]
    return onward, [(b, a) for a, b in onward]


def shift(block, axis, distance):
    count = lax.axis_size(axis)
    return lax.ppermute(block, axis, [(i, (i + distance) % count) for i in range(count)])


def swap(block, axis):
    return lax.ppermute(block, axis, [(0, 1), (1, 0)])


def tie(block, *others):
    return lax.optimization_barrier((block, *others))[0]


def first_part(t):
    return t * 5 // 8 // 16 * 16


def flip(block, axis, bit):
    return lax.ppermute(block, axis, [(i, i ^ bit) for i in range(lax.axis_size(axis))])


def ring_gather(block, axis, ahead):
    count = lax.axis_size(axis)
    onward, back = ring_routes(count)
    half = block.shape[0] // 2
    pieces = [(block, 0, 0)]
    left = right = block
    for step in range(1, count // 2):
        if step == 2:
            left, right, *_ = lax.optimization_barrier((left, right, *ahead))
        left = lax.ppermute(left, axis, onward)
        right = lax.ppermute(right, axis, back)
        pieces.append((left, -step, 0))
        pieces.append((right, step, 0))
    pieces.append((lax.ppermute(left[:half], axis, onward), count // 2, 0))
    pieces.append((lax.ppermute(right[half:], axis, back), count // 2, half))
    return pieces


def join_kernel(tokens, cotangent, both):
    t = tokens.shape[0]
    both[:t] = tokens[...]
    both[t:] = cotangent[...]


def join(tokens, cotangent):
    t, width = tokens.shape
    return pl.pallas_call(
        join_kernel,
        out_shape=shape((2 * t, width)),
        in_specs=[VMEM] * 2,
        out_specs=VMEM,
        compiler_params=params(),
        name="join",
        cost_estimate=cost(2),
    )(tokens, cotangent)


def pack_kernel(grid, gd, ud, dd, gr, ur, dr, gate, up, down, after, *refs):
    own = refs[0]
    sends = refs[1:SPREAD]
    slab, ids, used = refs[SPREAD:]
    me = lax.axis_index("fsdp")
    quarter = 2 * lax.axis_index("groups") + lax.axis_index("section")
    rows = BLK // 4
    slab[...] = jnp.zeros_like(slab)
    own[...] = jnp.zeros_like(own)
    ids[...] = jnp.zeros_like(ids)
    for kind, (dest, row_ids, blocks) in enumerate(((gd, gr, gate), (ud, ur, up), (dd, dr, down))):
        for offset in range(SPREAD):
            used[offset] = 0

        def place(j, carry, kind=kind, dest=dest, row_ids=row_ids, blocks=blocks):
            offset = dest[j]
            if grid:
                offset = me ^ lax.rem(me - offset + SPREAD, SPREAD)
            rank = used[offset]
            used[offset] = rank + 1
            slot = kind * CAP + rank
            start = pl.multiple_of(quarter * rows, rows)
            slab[offset, slot] = blocks[j, pl.ds(start, rows), :]
            ids[offset, pl.ds(slot, 1), :] = jnp.full((1, BLK), row_ids[j].astype(F32), F32)

            @pl.when(offset == 0)
            def _():
                own[slot] = blocks[j]

            return carry

        lax.fori_loop(0, blocks.shape[0], place, 0)
    for offset in range(1, SPREAD):
        sends[offset - 1][0:PER] = slab[offset]
        sends[offset - 1][PER] = ids[offset].astype(BF16)
    own[PER, 0:rows] = ids[0].astype(BF16)


def pack(grid, dests, row_ids, blocks, after):
    rows = BLK // 4
    return pl.pallas_call(
        functools.partial(pack_kernel, grid),
        out_shape=[shape((PER + 1, BLK, BLK))] + [shape((PER + 1, rows, BLK))] * (SPREAD - 1),
        in_specs=[SMEM] * 6 + [VMEM] * 3 + [ANY],
        out_specs=[VMEM] * SPREAD,
        scratch_shapes=[
            pltpu.VMEM((SPREAD, PER, rows, BLK), BF16),
            pltpu.VMEM((SPREAD, rows, BLK), F32),
            pltpu.SMEM((SPREAD,), jnp.int32),
        ],
        compiler_params=params(),
        name="pack",
        cost_estimate=cost(3),
    )(*dests, *row_ids, *blocks, after)


def forward_kernel(layout, tokens_here, split, own, w0, w1, w2, w3, *refs):
    count = len(layout)
    shards = refs[:count]
    refs = refs[count:]
    field_out, hidden_out = refs[0], refs[1]
    outs = refs[2 : 3 + 3 * split]
    field, weights, id_rows, id_ints, id_scalars, left, total, shard_sems, sems = refs[3 + 3 * split :]
    width = field.shape[2]
    per_piece = width // BLK
    t = tokens_here
    axis_size = lax.axis_size("fsdp")
    me = lax.axis_index("fsdp")
    group = lax.axis_index("groups")
    section = lax.axis_index("section")
    quarters = (
        2 * group + section,
        2 * group + 1 - section,
        2 * (1 - group) + section,
        2 * (1 - group) + 1 - section,
    )

    own_copies = [
        pltpu.make_async_copy(own.at[0:PER], weights.at[0], sems.at[0]),
        pltpu.make_async_copy(own.at[PER, 0 : BLK // 4], id_rows.at[0], sems.at[1]),
        pltpu.make_async_copy(w0.at[:, PER], id_rows.at[1:SPREAD], sems.at[2]),
    ]
    weight_copies = []
    for n, ref in enumerate((w0, w1, w2, w3)):
        begin = pl.multiple_of(quarters[n] * (BLK // 4), BLK // 4)
        weight_copies.append(
            pltpu.make_async_copy(
                ref.at[:, 0:PER],
                weights.at[1:SPREAD, :, pl.ds(begin, BLK // 4), :],
                sems.at[3 + n],
            )
        )
    shard_copies = []
    for n, (steps, first, length) in enumerate(layout):
        piece = ring_at(ring_place(me, axis_size) + steps, axis_size) if split else 0
        shard_copies.append(
            pltpu.make_async_copy(
                shards[n], field.at[piece, first : first + length], shard_sems.at[n]
            )
        )
    for copy in own_copies + shard_copies + weight_copies:
        copy.start()
    total[...] = jnp.zeros_like(total)
    for copy in own_copies[1:]:
        copy.wait()
    id_ints[...] = id_rows[:, 0:16, :].astype(F32).astype(jnp.int32)
    id_copy = pltpu.make_async_copy(id_ints, id_scalars, sems.at[7])
    id_copy.start()
    for copy in shard_copies:
        copy.wait()
    field_copy = pltpu.make_async_copy(field, field_out, sems.at[8])
    field_copy.start()
    id_copy.wait()

    def where(offset, kind, rank):
        row = id_scalars[offset, kind * CAP + rank, 0]
        return row // per_piece, pl.multiple_of((row % per_piece) * BLK, BLK)

    for kind in range(KINDS):
        first = t if kind == 2 else 0
        for offset in range(SPREAD):
            for rank in range(CAP):
                piece, column = where(offset, kind, rank)
                n = offset * CAP + rank
                left[kind, :, n * BLK : (n + 1) * BLK] = field[
                    piece, first : first + t, pl.ds(column, BLK)
                ]
    own_copies[0].wait()
    for copy in weight_copies:
        copy.wait()

    def block_group(kind):
        return weights[:, kind * CAP : (kind + 1) * CAP].reshape(SPREAD * CAP * BLK, BLK)

    gate = jnp.dot(left[0], block_group(0), preferred_element_type=F32)
    upper = jnp.dot(left[1], block_group(1), preferred_element_type=F32)
    nt = (((1,), (1,)), ((), ()))
    hidden_grad = jnp.zeros((t, BLK), F32)
    for offset in range(SPREAD):
        for rank in range(CAP):
            n = offset * CAP + rank
            hidden_grad = hidden_grad + lax.dot_general(
                left[2, :, n * BLK : (n + 1) * BLK],
                weights[offset, 2 * CAP + rank],
                nt,
                preferred_element_type=F32,
            )
    sigma = 1.0 / (1.0 + jnp.exp(-gate))
    hidden = (gate * sigma * upper).astype(BF16)
    gate_d = (hidden_grad * upper * sigma * (1.0 + gate * (1.0 - sigma))).astype(BF16)
    up_d = (hidden_grad * gate * sigma).astype(BF16)
    hidden_out[0] = gate_d
    hidden_out[1] = up_d
    hidden_out[2] = hidden
    for kind, grad in ((0, gate_d), (1, up_d)):
        for offset in range(SPREAD):
            terms = lax.dot_general(
                grad,
                weights[offset, kind * CAP : (kind + 1) * CAP].reshape(CAP * BLK, BLK),
                nt,
                preferred_element_type=F32,
            )
            for rank in range(CAP):
                piece, column = where(offset, kind, rank)
                total[piece, :, pl.ds(column, BLK)] += terms[:, rank * BLK : (rank + 1) * BLK]
    if split:
        h = first_part(t)
        send_a, send_b, keep_a, keep_b = outs
        for high in range(2):
            for low in range(2):
                a = me ^ (2 * high + 4 * low)
                b = me ^ (4 * high + low)
                n = 2 * high + low
                send_a[n] = total[a ^ 1, :h].astype(BF16)
                keep_a[n] = total[a, :h].astype(BF16)
                send_b[n] = total[b ^ 2, h:].astype(BF16)
                keep_b[n] = total[b, h:].astype(BF16)
    else:
        outs[0][...] = total[...].astype(BF16)
    field_copy.wait()


def forward(own, quarters, pieces, split, piece_count):
    layout = [(steps, first, block.shape[0]) for block, steps, first in pieces]
    t = pieces[0][0].shape[0] // 2
    width = pieces[0][0].shape[1]
    if split:
        rows = first_part(t), t - first_part(t)
        outs = [shape((piece_count // 2, rows[n % 2], width)) for n in range(4)]
    else:
        outs = [shape((piece_count, t, width))]
    field = (piece_count, 2 * t, width)
    return pl.pallas_call(
        functools.partial(forward_kernel, layout, t, int(split)),
        out_shape=[shape(field), shape((KINDS, t, BLK))] + outs,
        in_specs=[ANY] * (5 + len(pieces)),
        out_specs=[ANY] + [VMEM] * (1 + len(outs)),
        scratch_shapes=[
            pltpu.VMEM(field, BF16),
            pltpu.VMEM((SPREAD, PER, BLK, BLK), BF16),
            pltpu.VMEM((SPREAD, BLK // 4, BLK), BF16),
            pltpu.VMEM((SPREAD, 16, BLK), jnp.int32),
            pltpu.SMEM((SPREAD, 16, BLK), jnp.int32),
            pltpu.VMEM((KINDS, t, SPREAD * CAP * BLK), BF16),
            pltpu.VMEM((piece_count, t, width), F32),
            pltpu.SemaphoreType.DMA((len(pieces),)),
            pltpu.SemaphoreType.DMA((9,)),
        ],
        compiler_params=params(),
        name="forward",
        cost_estimate=cost(8),
    )(own, *quarters, *[block for block, _, _ in pieces])


def grads_kernel(layout, grid, gd, ud, dd, gr, ur, dr, field, *refs):
    out, columns, sems = refs[-3:]
    axis_size = lax.axis_size("fsdp")
    me = lax.axis_index("fsdp")
    t = field.shape[1] // 2
    per_piece = field.shape[2] // BLK
    copies = []
    for n, (array, row, away) in enumerate(layout):
        offset = (me - (me ^ away) + axis_size) % axis_size if grid else away
        copies.append(
            pltpu.make_async_copy(refs[array].at[row], columns.at[offset], sems.at[n])
        )
    for copy in copies:
        copy.start()
    for copy in copies:
        copy.wait()
    tn = (((0,), (0,)), ((), ()))
    slots = gd.shape[0]
    for kind, (dest, row_ids) in enumerate(((gd, gr), (ud, ur), (dd, dr))):
        first = t if kind == 2 else 0

        def one(j, carry, kind=kind, dest=dest, row_ids=row_ids, first=first):
            row = row_ids[j]
            column = pl.multiple_of((row % per_piece) * BLK, BLK)
            part = field[row // per_piece, first : first + t, pl.ds(column, BLK)]
            side = columns[dest[j], kind * t : (kind + 1) * t, :]
            pair_of = (side, part) if kind == 2 else (part, side)
            out[kind * slots + j] = lax.dot_general(
                *pair_of, tn, preferred_element_type=F32
            ).astype(BF16)
            return carry

        lax.fori_loop(0, slots, one, 0, unroll=4)


def grads(dests, row_ids, field, arrived, layout, grid, after):
    rows = arrived[0].shape[1]
    slots = dests[0].shape[0]
    return pl.pallas_call(
        functools.partial(grads_kernel, layout, grid),
        out_shape=shape((KINDS * slots, BLK, BLK)),
        in_specs=[SMEM] * 2 * KINDS + [VMEM] + [ANY] * (len(arrived) + len(after)),
        out_specs=VMEM,
        scratch_shapes=[
            pltpu.VMEM((SPREAD, rows, BLK), BF16),
            pltpu.SemaphoreType.DMA((SPREAD,)),
        ],
        compiler_params=params(),
        name="grads",
        cost_estimate=cost(7.5),
    )(*dests, *row_ids, field, *arrived, *after)


def shards(
    tokens,
    cotangent,
    gate_blocks,
    up_blocks,
    down_blocks,
    gate_dest,
    up_dest,
    down_dest,
    gate_rows,
    up_rows,
    down_rows,
):
    count = lax.axis_size("fsdp")
    grid = count == SPREAD and tokens.shape[1] % BLK == 0
    t = tokens.shape[0]
    dests = [target[:, 0] for target in (gate_dest, up_dest, down_dest)]
    row_ids = [gate_rows, up_rows, down_rows]

    both = join(tokens, cotangent)
    own, *sends = pack(grid, dests, row_ids, (gate_blocks, up_blocks, down_blocks), both)
    if grid:
        pieces = ring_gather(both, "fsdp", sends)
        first_step, second_step = ([block for block, _, _ in pieces[n : n + 2]] for n in (1, 3))
        sends = lax.optimization_barrier((*sends, *first_step))[:-2]
        slabs = [flip(block, "fsdp", bits) for bits, block in enumerate(sends, 1)]
        slabs = lax.optimization_barrier((*slabs, *second_step))[:-2]
        piece_count = count
    else:
        pieces = [(lax.all_gather(both, "fsdp", axis=1, tiled=True), 0, 0)]
        slabs = [shift(block, "fsdp", -d) for d, block in enumerate(sends, 1)]
        piece_count = 1

    mine = jnp.stack(slabs, axis=0)
    across = swap(mine, "groups")
    beside = swap(mine, "section")
    diagonal = swap(across, "section")
    quarters = (mine, beside, across, diagonal)
    field, columns, *partial_input = forward(own, quarters, pieces, grid, piece_count)
    flat = columns.reshape(1, KINDS * t, BLK)

    if grid:
        send_a, send_b, keep_a, keep_b = partial_input
        got_a = flip(send_a, "fsdp", 1)
        got_b = flip(send_b, "fsdp", 2)
        two = jnp.concatenate([flat, flip(flat, "fsdp", 4)], axis=0)
        four = jnp.concatenate([two, flip(two, "fsdp", 2)], axis=0)
        four, got_b = lax.optimization_barrier((four, got_b))
        rest = flip(four, "fsdp", 1)
        sum_b = keep_b + got_b
        away_b = tie(sum_b[2:])
        got_b = flip(away_b, "fsdp", 4)
        sum_a = keep_a + got_a
        away_a = tie(sum_a[2:])
        got_a = flip(away_a, "fsdp", 2)
        arrived = [four, rest]
        layout = [(n, row, n + bits) for n in range(2) for row, bits in enumerate((0, 4, 2, 6))]
        part = grads(dests, row_ids, field, arrived, layout, grid, [away_a, away_b])
        got_a, got_b, part = lax.optimization_barrier((got_a, got_b, part))
        sum_a = sum_a[:2] + got_a
        away_a = tie(sum_a[1:])
        got_a = flip(away_a, "fsdp", 4)
        part = tie(part, away_a)
        sum_b = sum_b[:2] + got_b
        got_b = flip(sum_b[1:], "fsdp", 1)
        input_grad = jnp.concatenate([sum_a[0] + got_a[0], sum_b[0] + got_b[0]], axis=0)
    else:
        input_grad = lax.psum_scatter(
            partial_input[0].reshape(t, -1), "fsdp", scatter_dimension=1, tiled=True
        )
        arrived = [flat] + [shift(flat, "fsdp", d) for d in range(1, SPREAD)]
        layout = [(d, 0, d) for d in range(SPREAD)]
        part = grads(dests, row_ids, field, arrived, layout, grid, [])
    slots = gate_blocks.shape[0]
    other = swap(part, "section")
    summed = part.astype(F32) + other.astype(F32)
    gate_grad, up_grad, down_grad = (
        summed[kind * slots : (kind + 1) * slots] for kind in range(KINDS)
    )
    return input_grad, gate_grad, up_grad, down_grad


def solution(mesh):
    return jax.shard_map(
        shards,
        mesh=mesh,
        in_specs=(
            P(("groups", "section"), "fsdp"),
            P(("groups", "section"), "fsdp"),
            P("fsdp", None, None),
            P("fsdp", None, None),
            P("fsdp", None, None),
            P("fsdp", None),
            P("fsdp", None),
            P("fsdp", None),
            P("fsdp"),
            P("fsdp"),
            P("fsdp"),
        ),
        out_specs=(
            P(("groups", "section"), "fsdp"),
            P(("groups", "fsdp"), None, None),
            P(("groups", "fsdp"), None, None),
            P(("groups", "fsdp"), None, None),
        ),
        check_vma=False,
    )
```

```python
import functools

import jax
import jax.numpy as jnp
from jax import lax
from jax.experimental import pallas as pl
from jax.experimental.pallas import tpu as pltpu
from jax.sharding import PartitionSpec as P

BLK = 128
SPREAD = 8
CAP = 3
KINDS = 3
PER = KINDS * CAP
EARLY = (4, 5, 1, 2)
BEFORE_THIRD = ()
MIB = 1024 * 1024

F32 = jnp.float32
BF16 = jnp.bfloat16
ANY = pl.BlockSpec(memory_space=pl.ANY)
VMEM = pl.BlockSpec(memory_space=pltpu.VMEM)
SMEM = pl.BlockSpec(memory_space=pltpu.SMEM)


def params(mebibytes):
    return pltpu.CompilerParams(vmem_limit_bytes=mebibytes * MIB)


def cost(micros):
    return pl.CostEstimate(flops=0, bytes_accessed=int(micros * 3.5e6), transcendentals=0)


def shape(dims, dtype=BF16):
    return jax.ShapeDtypeStruct(dims, dtype)


def near(arrays):
    return [pltpu.with_memory_space_constraint(array, pltpu.VMEM) for array in arrays]


def ring_at(place, count):
    place = place % count
    return jnp.where(place < count // 2, 2 * place, 2 * (count - 1 - place) + 1)


def ring_place(index, count):
    return jnp.where(index % 2 == 0, index // 2, count - 1 - index // 2)


def ring_routes(count):
    order = [*range(0, count, 2), *range(count - 1, 0, -2)]
    onward = [(order[i], order[(i + 1) % count]) for i in range(count)]
    return onward, [(b, a) for a, b in onward]


def shift(block, axis, distance):
    count = lax.axis_size(axis)
    return lax.ppermute(block, axis, [(i, (i + distance) % count) for i in range(count)])


def swap(block, axis):
    return lax.ppermute(block, axis, [(0, 1), (1, 0)])


def tie(block, *others):
    return lax.optimization_barrier((block, *others))[0]


def first_part(t):
    return t * 5 // 8 // 16 * 16


def flip(block, axis, bit):
    return lax.ppermute(block, axis, [(i, i ^ bit) for i in range(lax.axis_size(axis))])


def ring_step(left, right, axis):
    onward, back = ring_routes(lax.axis_size(axis))
    return lax.ppermute(left, axis, onward), lax.ppermute(right, axis, back)


def join_kernel(tokens, cotangent, both):
    t = tokens.shape[0]
    both[:t] = tokens[...]
    both[t:] = cotangent[...]


def join(tokens, cotangent):
    t, width = tokens.shape
    return pl.pallas_call(
        join_kernel,
        out_shape=shape((2 * t, width)),
        in_specs=[VMEM] * 2,
        out_specs=VMEM,
        compiler_params=params(56),
        name="join",
        cost_estimate=cost(2),
    )(tokens, cotangent)


def pack_kernel(grid, gd, ud, dd, gr, ur, dr, gate, up, down, after, *refs):
    own = refs[0]
    sends = refs[1:SPREAD]
    slab, ids, used = refs[SPREAD:]
    me = lax.axis_index("fsdp")
    quarter = 2 * lax.axis_index("groups") + lax.axis_index("section")
    rows = BLK // 4
    slab[...] = jnp.zeros_like(slab)
    own[...] = jnp.zeros_like(own)
    ids[...] = jnp.zeros_like(ids)
    for kind, (dest, row_ids, blocks) in enumerate(((gd, gr, gate), (ud, ur, up), (dd, dr, down))):
        for offset in range(SPREAD):
            used[offset] = 0

        def place(j, carry, kind=kind, dest=dest, row_ids=row_ids, blocks=blocks):
            offset = dest[j]
            if grid:
                offset = me ^ lax.rem(me - offset + SPREAD, SPREAD)
            rank = used[offset]
            used[offset] = rank + 1
            slot = kind * CAP + rank
            start = pl.multiple_of(quarter * rows, rows)
            slab[offset, slot] = blocks[j, pl.ds(start, rows), :]
            ids[offset, pl.ds(slot, 1), :] = jnp.full((1, BLK), row_ids[j].astype(F32), F32)

            @pl.when(offset == 0)
            def _():
                own[slot] = blocks[j]

            return carry

        lax.fori_loop(0, blocks.shape[0], place, 0)
    for offset in range(1, SPREAD):
        sends[offset - 1][0:PER] = slab[offset]
        sends[offset - 1][PER] = ids[offset].astype(BF16)
    own[PER, 0:rows] = ids[0].astype(BF16)


def pack(grid, dests, row_ids, blocks, after):
    rows = BLK // 4
    return pl.pallas_call(
        functools.partial(pack_kernel, grid),
        out_shape=[shape((PER + 1, BLK, BLK))] + [shape((PER + 1, rows, BLK))] * (SPREAD - 1),
        in_specs=[SMEM] * 6 + [VMEM] * 3 + [ANY],
        out_specs=[VMEM] * SPREAD,
        scratch_shapes=[
            pltpu.VMEM((SPREAD, PER, rows, BLK), BF16),
            pltpu.VMEM((SPREAD, rows, BLK), F32),
            pltpu.SMEM((SPREAD,), jnp.int32),
        ],
        compiler_params=params(56),
        name="pack",
        cost_estimate=cost(3),
    )(*dests, *row_ids, *blocks, after)


def forward_kernel(layout, tokens_here, split, own, w0, w1, w2, w3, *refs):
    count = len(layout)
    shards = refs[:count]
    refs = refs[count:]
    field_out, hidden_out = refs[0], refs[1]
    outs = refs[2 : 3 + 3 * split]
    field, weights, id_rows, id_ints, id_scalars, left, total, shard_sems, sems = refs[3 + 3 * split :]
    width = field.shape[2]
    per_piece = width // BLK
    t = tokens_here
    axis_size = lax.axis_size("fsdp")
    me = lax.axis_index("fsdp")
    group = lax.axis_index("groups")
    section = lax.axis_index("section")
    quarters = (
        2 * group + section,
        2 * group + 1 - section,
        2 * (1 - group) + section,
        2 * (1 - group) + 1 - section,
    )

    own_copies = [
        pltpu.make_async_copy(own.at[0:PER], weights.at[0], sems.at[0]),
        pltpu.make_async_copy(own.at[PER, 0 : BLK // 4], id_rows.at[0], sems.at[1]),
        pltpu.make_async_copy(w0.at[:, PER], id_rows.at[1:SPREAD], sems.at[2]),
    ]
    weight_copies = []
    for n, ref in enumerate((w0, w1, w2, w3)):
        begin = pl.multiple_of(quarters[n] * (BLK // 4), BLK // 4)
        weight_copies.append(
            pltpu.make_async_copy(
                ref.at[:, 0:PER],
                weights.at[1:SPREAD, :, pl.ds(begin, BLK // 4), :],
                sems.at[3 + n],
            )
        )
    shard_copies = []
    for n, (steps, first, length) in enumerate(layout):
        piece = ring_at(ring_place(me, axis_size) + steps, axis_size) if split else 0
        shard_copies.append(
            pltpu.make_async_copy(
                shards[n], field.at[piece, first : first + length], shard_sems.at[n]
            )
        )
    for copy in own_copies + shard_copies + weight_copies:
        copy.start()
    total[...] = jnp.zeros_like(total)
    for copy in own_copies[1:]:
        copy.wait()
    id_ints[...] = id_rows[:, 0:16, :].astype(F32).astype(jnp.int32)
    id_copy = pltpu.make_async_copy(id_ints, id_scalars, sems.at[7])
    id_copy.start()
    for copy in shard_copies:
        copy.wait()
    field_copy = pltpu.make_async_copy(field, field_out, sems.at[8])
    field_copy.start()
    id_copy.wait()

    def where(offset, kind, rank):
        row = id_scalars[offset, kind * CAP + rank, 0]
        return row // per_piece, pl.multiple_of((row % per_piece) * BLK, BLK)

    for kind in range(KINDS):
        first = t if kind == 2 else 0
        for offset in range(SPREAD):
            for rank in range(CAP):
                piece, column = where(offset, kind, rank)
                n = offset * CAP + rank
                left[kind, :, n * BLK : (n + 1) * BLK] = field[
                    piece, first : first + t, pl.ds(column, BLK)
                ]
    own_copies[0].wait()
    for copy in weight_copies:
        copy.wait()

    def block_group(kind):
        return weights[:, kind * CAP : (kind + 1) * CAP].reshape(SPREAD * CAP * BLK, BLK)

    gate = jnp.dot(left[0], block_group(0), preferred_element_type=F32)
    upper = jnp.dot(left[1], block_group(1), preferred_element_type=F32)
    nt = (((1,), (1,)), ((), ()))
    across = jnp.concatenate(
        [weights[n // CAP, 2 * CAP + n % CAP] for n in range(SPREAD * CAP)], axis=1
    )
    hidden_grad = lax.dot_general(left[2], across, nt, preferred_element_type=F32)
    sigma = 1.0 / (1.0 + jnp.exp(-gate))
    hidden = (gate * sigma * upper).astype(BF16)
    gate_d = (hidden_grad * upper * sigma * (1.0 + gate * (1.0 - sigma))).astype(BF16)
    up_d = (hidden_grad * gate * sigma).astype(BF16)
    hidden_out[0] = gate_d
    hidden_out[1] = up_d
    hidden_out[2] = hidden
    for kind, grad in ((0, gate_d), (1, up_d)):
        for offset in range(SPREAD):
            terms = lax.dot_general(
                grad,
                weights[offset, kind * CAP : (kind + 1) * CAP].reshape(CAP * BLK, BLK),
                nt,
                preferred_element_type=F32,
            )
            for rank in range(CAP):
                piece, column = where(offset, kind, rank)
                total[piece, :, pl.ds(column, BLK)] += terms[:, rank * BLK : (rank + 1) * BLK]
    if split:
        h = first_part(t)
        send_a, send_b, keep_a, keep_b = outs
        for high in range(2):
            for low in range(2):
                a = me ^ (2 * high + 4 * low)
                b = me ^ (4 * high + low)
                n = 2 * high + low
                send_a[n] = total[a ^ 1, :h].astype(BF16)
                keep_a[n] = total[a, :h].astype(BF16)
                send_b[n] = total[b ^ 2, h:].astype(BF16)
                keep_b[n] = total[b, h:].astype(BF16)
    else:
        outs[0][...] = total[...].astype(BF16)
    field_copy.wait()


def forward(own, quarters, pieces, split, piece_count):
    layout = [(steps, first, block.shape[0]) for block, steps, first in pieces]
    t = pieces[0][0].shape[0] // 2
    width = pieces[0][0].shape[1]
    if split:
        rows = first_part(t), t - first_part(t)
        outs = [shape((piece_count // 2, rows[n % 2], width)) for n in range(4)]
    else:
        outs = [shape((piece_count, t, width))]
    field = (piece_count, 2 * t, width)
    return pl.pallas_call(
        functools.partial(forward_kernel, layout, t, int(split)),
        out_shape=[shape(field), shape((KINDS, t, BLK))] + outs,
        in_specs=[ANY] * (5 + len(pieces)),
        out_specs=[ANY] + [VMEM] * (1 + len(outs)),
        scratch_shapes=[
            pltpu.VMEM(field, BF16),
            pltpu.VMEM((SPREAD, PER, BLK, BLK), BF16),
            pltpu.VMEM((SPREAD, BLK // 4, BLK), BF16),
            pltpu.VMEM((SPREAD, 16, BLK), jnp.int32),
            pltpu.SMEM((SPREAD, 16, BLK), jnp.int32),
            pltpu.VMEM((KINDS, t, SPREAD * CAP * BLK), BF16),
            pltpu.VMEM((piece_count, t, width), F32),
            pltpu.SemaphoreType.DMA((len(pieces),)),
            pltpu.SemaphoreType.DMA((9,)),
        ],
        compiler_params=params(32),
        name="forward",
        cost_estimate=cost(8),
    )(own, *(near if split else list)([*quarters, *[block for block, _, _ in pieces]]))


def grads_kernel(layout, grid, gd, ud, dd, gr, ur, dr, field, *refs):
    out, columns, sems = refs[-3:]
    axis_size = lax.axis_size("fsdp")
    me = lax.axis_index("fsdp")
    t = field.shape[1] // 2
    per_piece = field.shape[2] // BLK
    copies = []
    for n, (array, row, away) in enumerate(layout):
        offset = (me - (me ^ away) + axis_size) % axis_size if grid else away
        copies.append(
            pltpu.make_async_copy(refs[array].at[row], columns.at[offset], sems.at[n])
        )
    for copy in copies:
        copy.start()
    for copy in copies:
        copy.wait()
    tn = (((0,), (0,)), ((), ()))
    slots = gd.shape[0]
    for kind, (dest, row_ids) in enumerate(((gd, gr), (ud, ur), (dd, dr))):
        first = t if kind == 2 else 0

        def one(j, carry, kind=kind, dest=dest, row_ids=row_ids, first=first):
            row = row_ids[j]
            column = pl.multiple_of((row % per_piece) * BLK, BLK)
            part = field[row // per_piece, first : first + t, pl.ds(column, BLK)]
            side = columns[dest[j], kind * t : (kind + 1) * t, :]
            pair_of = (side, part) if kind == 2 else (part, side)
            out[kind * slots + j] = lax.dot_general(
                *pair_of, tn, preferred_element_type=F32
            ).astype(BF16)
            return carry

        lax.fori_loop(0, slots, one, 0, unroll=16)


def grads(dests, row_ids, field, arrived, layout, grid, after):
    rows = arrived[0].shape[1]
    slots = dests[0].shape[0]
    return pl.pallas_call(
        functools.partial(grads_kernel, layout, grid),
        out_shape=shape((KINDS * slots, BLK, BLK)),
        in_specs=[SMEM] * 2 * KINDS + [VMEM] + [ANY] * (len(arrived) + len(after)),
        out_specs=VMEM,
        scratch_shapes=[
            pltpu.VMEM((SPREAD, rows, BLK), BF16),
            pltpu.SemaphoreType.DMA((SPREAD,)),
        ],
        compiler_params=params(32),
        name="grads",
        cost_estimate=cost(7.5),
    )(*dests, *row_ids, field, *arrived, *after)


def shards(
    tokens,
    cotangent,
    gate_blocks,
    up_blocks,
    down_blocks,
    gate_dest,
    up_dest,
    down_dest,
    gate_rows,
    up_rows,
    down_rows,
):
    count = lax.axis_size("fsdp")
    grid = count == SPREAD and tokens.shape[1] % BLK == 0
    t = tokens.shape[0]
    dests = [target[:, 0] for target in (gate_dest, up_dest, down_dest)]
    row_ids = [gate_rows, up_rows, down_rows]

    both = join(tokens, cotangent)
    own, *sends = pack(grid, dests, row_ids, (gate_blocks, up_blocks, down_blocks), both)
    if grid:
        slabs = {}
        steps = [ring_step(both, both, "fsdp")]
        for bits in EARLY:
            slabs[bits] = flip(sends[bits - 1], "fsdp", bits)
        held = lax.optimization_barrier((*steps[0], *slabs.values()))
        steps.append(ring_step(*held[:2], "fsdp"))
        for bits in range(1, SPREAD):
            if bits not in EARLY:
                slabs[bits] = flip(tie(sends[bits - 1], *steps[0]), "fsdp", bits)
        held = lax.optimization_barrier((*steps[1], *[slabs[bits] for bits in BEFORE_THIRD]))
        steps.append(ring_step(*held[:2], "fsdp"))
        left, right = steps[2]
        steps.append(ring_step(left[:t], right[t:], "fsdp"))
        pieces = [(both, 0, 0)]
        for step, (left, right) in enumerate(steps, 1):
            pieces += [(left, -step, 0), (right, step, t if step == count // 2 else 0)]
        slabs = [slabs[bits] for bits in range(1, SPREAD)]
        slabs = lax.optimization_barrier((*slabs, *steps[1]))[:-2]
        piece_count = count
    else:
        pieces = [(lax.all_gather(both, "fsdp", axis=1, tiled=True), 0, 0)]
        slabs = [shift(block, "fsdp", -d) for d, block in enumerate(sends, 1)]
        piece_count = 1

    mine = jnp.stack(slabs, axis=0)
    across = swap(mine, "groups")
    beside = swap(mine, "section")
    diagonal = swap(across, "section")
    quarters = (mine, beside, across, diagonal)
    field, columns, *partial_input = forward(own, quarters, pieces, grid, piece_count)
    flat = columns.reshape(1, KINDS * t, BLK)

    if grid:
        send_a, send_b, keep_a, keep_b = partial_input
        got_a = flip(send_a, "fsdp", 1)
        got_b = flip(send_b, "fsdp", 2)
        two = jnp.concatenate([flat, flip(flat, "fsdp", 4)], axis=0)
        four = jnp.concatenate([two, flip(two, "fsdp", 2)], axis=0)
        four, got_b = lax.optimization_barrier((four, got_b))
        rest = flip(four, "fsdp", 1)
        sum_b = keep_b + got_b
        away_b = tie(sum_b[2:])
        got_b = flip(away_b, "fsdp", 4)
        sum_a = keep_a + got_a
        away_a = tie(sum_a[2:])
        got_a = flip(away_a, "fsdp", 2)
        arrived = [four, rest]
        layout = [(n, row, n + bits) for n in range(2) for row, bits in enumerate((0, 4, 2, 6))]
        part = grads(dests, row_ids, field, arrived, layout, grid, [away_a, away_b])
        got_a, got_b, part = lax.optimization_barrier((got_a, got_b, part))
        sum_a = sum_a[:2] + got_a
        away_a = tie(sum_a[1:])
        got_a = flip(away_a, "fsdp", 4)
        part = tie(part, away_a)
        sum_b = sum_b[:2] + got_b
        got_b = flip(sum_b[1:], "fsdp", 1)
        input_grad = jnp.concatenate([sum_a[0] + got_a[0], sum_b[0] + got_b[0]], axis=0)
    else:
        input_grad = lax.psum_scatter(
            partial_input[0].reshape(t, -1), "fsdp", scatter_dimension=1, tiled=True
        )
        arrived = [flat] + [shift(flat, "fsdp", d) for d in range(1, SPREAD)]
        layout = [(d, 0, d) for d in range(SPREAD)]
        part = grads(dests, row_ids, field, arrived, layout, grid, [])
    slots = gate_blocks.shape[0]
    other = swap(part, "section")
    summed = part.astype(F32) + other.astype(F32)
    gate_grad, up_grad, down_grad = (
        summed[kind * slots : (kind + 1) * slots] for kind in range(KINDS)
    )
    return input_grad, gate_grad, up_grad, down_grad


def solution(mesh):
    return jax.shard_map(
        shards,
        mesh=mesh,
        in_specs=(
            P(("groups", "section"), "fsdp"),
            P(("groups", "section"), "fsdp"),
            P("fsdp", None, None),
            P("fsdp", None, None),
            P("fsdp", None, None),
            P("fsdp", None),
            P("fsdp", None),
            P("fsdp", None),
            P("fsdp"),
            P("fsdp"),
            P("fsdp"),
        ),
        out_specs=(
            P(("groups", "section"), "fsdp"),
            P(("groups", "fsdp"), None, None),
            P(("groups", "fsdp"), None, None),
            P(("groups", "fsdp"), None, None),
        ),
        check_vma=False,
    )
```

```python
import functools

import jax
import jax.numpy as jnp
from jax import lax
from jax.experimental import pallas as pl
from jax.experimental.pallas import tpu as pltpu
from jax.sharding import PartitionSpec as P

BLK = 128
SPREAD = 8
CAP = 3
KINDS = 3
PER = KINDS * CAP
EARLY = (4, 7, 1, 2)
BEFORE_SECOND = (4, 7, 1, 2)
BEFORE_THIRD = ()
MIB = 1024 * 1024

F32 = jnp.float32
BF16 = jnp.bfloat16
ANY = pl.BlockSpec(memory_space=pl.ANY)
VMEM = pl.BlockSpec(memory_space=pltpu.VMEM)
SMEM = pl.BlockSpec(memory_space=pltpu.SMEM)


def params(mebibytes):
    return pltpu.CompilerParams(vmem_limit_bytes=mebibytes * MIB)


def cost(micros):
    return pl.CostEstimate(flops=0, bytes_accessed=int(micros * 3.5e6), transcendentals=0)


def shape(dims, dtype=BF16):
    return jax.ShapeDtypeStruct(dims, dtype)


def far(array):
    return pltpu.with_memory_space_constraint(array, pltpu.HBM)


def near(arrays):
    return [pltpu.with_memory_space_constraint(array, pltpu.VMEM) for array in arrays]


def ring_at(place, count):
    place = place % count
    return jnp.where(place < count // 2, 2 * place, 2 * (count - 1 - place) + 1)


def ring_place(index, count):
    return jnp.where(index % 2 == 0, index // 2, count - 1 - index // 2)


def ring_routes(count):
    order = [*range(0, count, 2), *range(count - 1, 0, -2)]
    onward = [(order[i], order[(i + 1) % count]) for i in range(count)]
    return onward, [(b, a) for a, b in onward]


def shift(block, axis, distance):
    count = lax.axis_size(axis)
    return lax.ppermute(block, axis, [(i, (i + distance) % count) for i in range(count)])


def swap(block, axis):
    return lax.ppermute(block, axis, [(0, 1), (1, 0)])


def tie(block, *others):
    return lax.optimization_barrier((block, *others))[0]


def first_part(t):
    return t * 5 // 8 // 16 * 16


def flip(block, axis, bit):
    return lax.ppermute(block, axis, [(i, i ^ bit) for i in range(lax.axis_size(axis))])


def ring_step(left, right, axis):
    onward, back = ring_routes(lax.axis_size(axis))
    return lax.ppermute(left, axis, onward), lax.ppermute(right, axis, back)


def join_kernel(tokens, cotangent, both):
    t = tokens.shape[0]
    both[:t] = tokens[...]
    both[t:] = cotangent[...]


def join(tokens, cotangent):
    t, width = tokens.shape
    return pl.pallas_call(
        join_kernel,
        out_shape=shape((2 * t, width)),
        in_specs=[VMEM] * 2,
        out_specs=VMEM,
        compiler_params=params(56),
        name="join",
        cost_estimate=cost(2),
    )(tokens, cotangent)


def pack_kernel(grid, gd, ud, dd, gr, ur, dr, gate, up, down, after, *refs):
    own = refs[0]
    sends = refs[1:SPREAD]
    slab, ids, used = refs[SPREAD:]
    me = lax.axis_index("fsdp")
    quarter = 2 * lax.axis_index("groups") + lax.axis_index("section")
    rows = BLK // 4
    slab[...] = jnp.zeros_like(slab)
    own[...] = jnp.zeros_like(own)
    ids[...] = jnp.zeros_like(ids)
    for kind, (dest, row_ids, blocks) in enumerate(((gd, gr, gate), (ud, ur, up), (dd, dr, down))):
        for offset in range(SPREAD):
            used[offset] = 0

        def place(j, carry, kind=kind, dest=dest, row_ids=row_ids, blocks=blocks):
            offset = dest[j]
            if grid:
                offset = me ^ lax.rem(me - offset + SPREAD, SPREAD)
            rank = used[offset]
            used[offset] = rank + 1
            slot = kind * CAP + rank
            start = pl.multiple_of(quarter * rows, rows)
            slab[offset, slot] = blocks[j, pl.ds(start, rows), :]
            ids[offset, pl.ds(slot, 1), :] = jnp.full((1, BLK), row_ids[j].astype(F32), F32)

            @pl.when(offset == 0)
            def _():
                own[slot] = blocks[j]

            return carry

        lax.fori_loop(0, blocks.shape[0], place, 0)
    for offset in range(1, SPREAD):
        sends[offset - 1][0:PER] = slab[offset]
        sends[offset - 1][PER] = ids[offset].astype(BF16)
    own[PER, 0:rows] = ids[0].astype(BF16)


def pack(grid, dests, row_ids, blocks, after):
    rows = BLK // 4
    return pl.pallas_call(
        functools.partial(pack_kernel, grid),
        out_shape=[shape((PER + 1, BLK, BLK))] + [shape((PER + 1, rows, BLK))] * (SPREAD - 1),
        in_specs=[SMEM] * 6 + [VMEM] * 3 + [ANY],
        out_specs=[VMEM] * SPREAD,
        scratch_shapes=[
            pltpu.VMEM((SPREAD, PER, rows, BLK), BF16),
            pltpu.VMEM((SPREAD, rows, BLK), F32),
            pltpu.SMEM((SPREAD,), jnp.int32),
        ],
        compiler_params=params(56),
        name="pack",
        cost_estimate=cost(3),
    )(*dests, *row_ids, *blocks, after)


def forward_kernel(layout, tokens_here, split, own, w0, w1, w2, w3, *refs):
    count = len(layout)
    shards = refs[:count]
    refs = refs[count:]
    field_out, hidden_out = refs[0], refs[1]
    outs = refs[2 : 3 + 3 * split]
    field, weights, id_rows, id_ints, id_scalars, left, total, shard_sems, sems = refs[3 + 3 * split :]
    width = field.shape[2]
    per_piece = width // BLK
    t = tokens_here
    axis_size = lax.axis_size("fsdp")
    me = lax.axis_index("fsdp")
    group = lax.axis_index("groups")
    section = lax.axis_index("section")
    quarters = (
        2 * group + section,
        2 * group + 1 - section,
        2 * (1 - group) + section,
        2 * (1 - group) + 1 - section,
    )

    own_copies = [
        pltpu.make_async_copy(own.at[0:PER], weights.at[0], sems.at[0]),
        pltpu.make_async_copy(own.at[PER, 0 : BLK // 4], id_rows.at[0], sems.at[1]),
        pltpu.make_async_copy(w0.at[:, PER], id_rows.at[1:SPREAD], sems.at[2]),
    ]
    weight_copies = []
    for n, ref in enumerate((w0, w1, w2, w3)):
        begin = pl.multiple_of(quarters[n] * (BLK // 4), BLK // 4)
        weight_copies.append(
            pltpu.make_async_copy(
                ref.at[:, 0:PER],
                weights.at[1:SPREAD, :, pl.ds(begin, BLK // 4), :],
                sems.at[3 + n],
            )
        )
    shard_copies = []
    for n, (steps, first, length) in enumerate(layout):
        piece = ring_at(ring_place(me, axis_size) + steps, axis_size) if split else 0
        shard_copies.append(
            pltpu.make_async_copy(
                shards[n], field.at[piece, first : first + length], shard_sems.at[n]
            )
        )
    for copy in own_copies + shard_copies + weight_copies:
        copy.start()
    total[...] = jnp.zeros_like(total)
    for copy in own_copies[1:]:
        copy.wait()
    id_ints[...] = id_rows[:, 0:16, :].astype(F32).astype(jnp.int32)
    id_copy = pltpu.make_async_copy(id_ints, id_scalars, sems.at[7])
    id_copy.start()
    for copy in shard_copies:
        copy.wait()
    field_copy = pltpu.make_async_copy(field, field_out, sems.at[8])
    field_copy.start()
    id_copy.wait()

    def where(offset, kind, rank):
        row = id_scalars[offset, kind * CAP + rank, 0]
        return row // per_piece, pl.multiple_of((row % per_piece) * BLK, BLK)

    for kind in range(KINDS):
        first = t if kind == 2 else 0
        for offset in range(SPREAD):
            for rank in range(CAP):
                piece, column = where(offset, kind, rank)
                n = offset * CAP + rank
                left[kind, :, n * BLK : (n + 1) * BLK] = field[
                    piece, first : first + t, pl.ds(column, BLK)
                ]
    own_copies[0].wait()
    for copy in weight_copies:
        copy.wait()

    def block_group(kind):
        return weights[:, kind * CAP : (kind + 1) * CAP].reshape(SPREAD * CAP * BLK, BLK)

    gate = jnp.dot(left[0], block_group(0), preferred_element_type=F32)
    upper = jnp.dot(left[1], block_group(1), preferred_element_type=F32)
    nt = (((1,), (1,)), ((), ()))
    across = jnp.concatenate(
        [weights[n // CAP, 2 * CAP + n % CAP] for n in range(SPREAD * CAP)], axis=1
    )
    hidden_grad = lax.dot_general(left[2], across, nt, preferred_element_type=F32)
    sigma = 1.0 / (1.0 + jnp.exp(-gate))
    hidden = (gate * sigma * upper).astype(BF16)
    gate_d = (hidden_grad * upper * sigma * (1.0 + gate * (1.0 - sigma))).astype(BF16)
    up_d = (hidden_grad * gate * sigma).astype(BF16)
    hidden_out[0] = gate_d
    hidden_out[1] = up_d
    hidden_out[2] = hidden
    for kind, grad in ((0, gate_d), (1, up_d)):
        for offset in range(SPREAD):
            terms = lax.dot_general(
                grad,
                weights[offset, kind * CAP : (kind + 1) * CAP].reshape(CAP * BLK, BLK),
                nt,
                preferred_element_type=F32,
            )
            for rank in range(CAP):
                piece, column = where(offset, kind, rank)
                total[piece, :, pl.ds(column, BLK)] += terms[:, rank * BLK : (rank + 1) * BLK]
    if split:
        h = first_part(t)
        send_a, send_b, keep_a, keep_b = outs
        for high in range(2):
            for low in range(2):
                a = me ^ (2 * high + 4 * low)
                b = me ^ (4 * high + low)
                n = 2 * high + low
                send_a[n] = total[a ^ 1, :h].astype(BF16)
                keep_a[n] = total[a, :h].astype(BF16)
                send_b[n] = total[b ^ 2, h:].astype(BF16)
                keep_b[n] = total[b, h:].astype(BF16)
    else:
        outs[0][...] = total[...].astype(BF16)
    field_copy.wait()


def forward(own, quarters, pieces, split, piece_count):
    layout = [(steps, first, block.shape[0]) for block, steps, first in pieces]
    t = pieces[0][0].shape[0] // 2
    width = pieces[0][0].shape[1]
    if split:
        rows = first_part(t), t - first_part(t)
        outs = [shape((piece_count // 2, rows[n % 2], width)) for n in range(4)]
    else:
        outs = [shape((piece_count, t, width))]
    field = (piece_count, 2 * t, width)
    return pl.pallas_call(
        functools.partial(forward_kernel, layout, t, int(split)),
        out_shape=[shape(field), shape((KINDS, t, BLK))] + outs,
        in_specs=[ANY] * (5 + len(pieces)),
        out_specs=[ANY] + [VMEM] * (1 + len(outs)),
        scratch_shapes=[
            pltpu.VMEM(field, BF16),
            pltpu.VMEM((SPREAD, PER, BLK, BLK), BF16),
            pltpu.VMEM((SPREAD, BLK // 4, BLK), BF16),
            pltpu.VMEM((SPREAD, 16, BLK), jnp.int32),
            pltpu.SMEM((SPREAD, 16, BLK), jnp.int32),
            pltpu.VMEM((KINDS, t, SPREAD * CAP * BLK), BF16),
            pltpu.VMEM((piece_count, t, width), F32),
            pltpu.SemaphoreType.DMA((len(pieces),)),
            pltpu.SemaphoreType.DMA((9,)),
        ],
        compiler_params=params(32),
        name="forward",
        cost_estimate=cost(8),
    )(far(own), *(near if split else list)([*quarters, *[block for block, _, _ in pieces]]))


def grads_kernel(layout, grid, gd, ud, dd, gr, ur, dr, field, *refs):
    out, columns, sems = refs[-3:]
    axis_size = lax.axis_size("fsdp")
    me = lax.axis_index("fsdp")
    t = field.shape[1] // 2
    per_piece = field.shape[2] // BLK
    copies = []
    for n, (array, row, away) in enumerate(layout):
        offset = (me - (me ^ away) + axis_size) % axis_size if grid else away
        copies.append(
            pltpu.make_async_copy(refs[array].at[row], columns.at[offset], sems.at[n])
        )
    for copy in copies:
        copy.start()
    for copy in copies:
        copy.wait()
    tn = (((0,), (0,)), ((), ()))
    slots = gd.shape[0]
    for kind, (dest, row_ids) in enumerate(((gd, gr), (ud, ur), (dd, dr))):
        first = t if kind == 2 else 0

        def one(j, carry, kind=kind, dest=dest, row_ids=row_ids, first=first):
            row = row_ids[j]
            column = pl.multiple_of((row % per_piece) * BLK, BLK)
            part = field[row // per_piece, first : first + t, pl.ds(column, BLK)]
            side = columns[dest[j], kind * t : (kind + 1) * t, :]
            pair_of = (side, part) if kind == 2 else (part, side)
            out[kind * slots + j] = lax.dot_general(
                *pair_of, tn, preferred_element_type=F32
            ).astype(BF16)
            return carry

        lax.fori_loop(0, slots, one, 0, unroll=16)


def grads(dests, row_ids, field, arrived, layout, grid, after):
    rows = arrived[0].shape[1]
    slots = dests[0].shape[0]
    return pl.pallas_call(
        functools.partial(grads_kernel, layout, grid),
        out_shape=shape((KINDS * slots, BLK, BLK)),
        in_specs=[SMEM] * 2 * KINDS + [VMEM] + [ANY] * (len(arrived) + len(after)),
        out_specs=VMEM,
        scratch_shapes=[
            pltpu.VMEM((SPREAD, rows, BLK), BF16),
            pltpu.SemaphoreType.DMA((SPREAD,)),
        ],
        compiler_params=params(32),
        name="grads",
        cost_estimate=cost(7.5),
    )(*dests, *row_ids, field, *arrived, *after)


def added(part, slots):
    other = swap(part, "section")
    summed = part.astype(F32) + other.astype(F32)
    return [summed[kind * slots : (kind + 1) * slots] for kind in range(KINDS)]


def shards(
    tokens,
    cotangent,
    gate_blocks,
    up_blocks,
    down_blocks,
    gate_dest,
    up_dest,
    down_dest,
    gate_rows,
    up_rows,
    down_rows,
):
    count = lax.axis_size("fsdp")
    grid = count == SPREAD and tokens.shape[1] % BLK == 0
    t = tokens.shape[0]
    slots = gate_blocks.shape[0]
    dests = [target[:, 0] for target in (gate_dest, up_dest, down_dest)]
    row_ids = [gate_rows, up_rows, down_rows]

    both = join(tokens, cotangent)
    own, *sends = pack(grid, dests, row_ids, (gate_blocks, up_blocks, down_blocks), both)
    if grid:
        slabs = {}
        steps = [ring_step(both, both, "fsdp")]
        for bits in EARLY:
            slabs[bits] = flip(sends[bits - 1], "fsdp", bits)
        held = lax.optimization_barrier((*steps[0], *[slabs[bits] for bits in BEFORE_SECOND]))
        steps.append(ring_step(*held[:2], "fsdp"))
        for bits in range(1, SPREAD):
            if bits not in EARLY:
                slabs[bits] = flip(tie(sends[bits - 1], *steps[0]), "fsdp", bits)
        held = lax.optimization_barrier((*steps[1], *[slabs[bits] for bits in BEFORE_THIRD]))
        steps.append(ring_step(*held[:2], "fsdp"))
        left, right = steps[2]
        steps.append(ring_step(left[:t], right[t:], "fsdp"))
        pieces = [(both, 0, 0)]
        for step, (left, right) in enumerate(steps, 1):
            pieces += [(left, -step, 0), (right, step, t if step == count // 2 else 0)]
        slabs = [slabs[bits] for bits in range(1, SPREAD)]
        slabs = lax.optimization_barrier((*slabs, *steps[1]))[:-2]
        piece_count = count
    else:
        pieces = [(lax.all_gather(both, "fsdp", axis=1, tiled=True), 0, 0)]
        slabs = [shift(block, "fsdp", -d) for d, block in enumerate(sends, 1)]
        piece_count = 1

    mine = jnp.stack(slabs, axis=0)
    across = swap(mine, "groups")
    beside = swap(mine, "section")
    diagonal = swap(across, "section")
    quarters = (mine, beside, across, diagonal)
    field, columns, *partial_input = forward(own, quarters, pieces, grid, piece_count)
    flat = columns.reshape(1, KINDS * t, BLK)

    if grid:
        send_a, send_b, keep_a, keep_b = partial_input
        got_a = flip(send_a, "fsdp", 1)
        two = jnp.concatenate([flat, flip(flat, "fsdp", 4)], axis=0)
        got_b = flip(tie(send_b, two), "fsdp", 2)
        beside = flip(two, "fsdp", 2)
        sum_a = keep_a + got_a
        away_a = tie(sum_a[2:])
        got_a = flip(away_a, "fsdp", 2)
        beside, away_a = lax.optimization_barrier((beside, away_a))
        four = jnp.concatenate([two, beside], axis=0)
        rest = flip(four, "fsdp", 1)
        sum_b = keep_b + got_b
        away_b = tie(sum_b[2:])
        got_b = flip(away_b, "fsdp", 4)
        arrived = [four, rest]
        layout = [(n, row, n + bits) for n in range(2) for row, bits in enumerate((0, 4, 2, 6))]
        part = grads(dests, row_ids, field, arrived, layout, grid, [away_a, away_b])
        got_a, part = lax.optimization_barrier((got_a, part))
        sum_a = sum_a[:2] + got_a
        away_a = tie(sum_a[1:])
        part, got_b, away_a = lax.optimization_barrier((part, got_b, away_a))
        got_a = flip(away_a, "fsdp", 4)
        sum_b = sum_b[:2] + got_b
        got_b = flip(sum_b[1:], "fsdp", 1)
        block_grads = added(part, slots)
        got_a, got_b, *block_grads = lax.optimization_barrier((got_a, got_b, *block_grads))
        input_grad = jnp.concatenate([sum_a[0] + got_a[0], sum_b[0] + got_b[0]], axis=0)
    else:
        input_grad = lax.psum_scatter(
            partial_input[0].reshape(t, -1), "fsdp", scatter_dimension=1, tiled=True
        )
        arrived = [flat] + [shift(flat, "fsdp", d) for d in range(1, SPREAD)]
        layout = [(d, 0, d) for d in range(SPREAD)]
        part = grads(dests, row_ids, field, arrived, layout, grid, [])
        block_grads = added(part, slots)
    return input_grad, *block_grads


def solution(mesh):
    return jax.shard_map(
        shards,
        mesh=mesh,
        in_specs=(
            P(("groups", "section"), "fsdp"),
            P(("groups", "section"), "fsdp"),
            P("fsdp", None, None),
            P("fsdp", None, None),
            P("fsdp", None, None),
            P("fsdp", None),
            P("fsdp", None),
            P("fsdp", None),
            P("fsdp"),
            P("fsdp"),
            P("fsdp"),
        ),
        out_specs=(
            P(("groups", "section"), "fsdp"),
            P(("groups", "fsdp"), None, None),
            P(("groups", "fsdp"), None, None),
            P(("groups", "fsdp"), None, None),
        ),
        check_vma=False,
    )
```

```python
import functools

import jax
import jax.numpy as jnp
from jax import lax
from jax.experimental import pallas as pl
from jax.experimental.pallas import tpu as pltpu
from jax.sharding import PartitionSpec as P

BLK = 128
SPREAD = 8
CAP = 3
KINDS = 3
PER = KINDS * CAP
PART = BLK // 4
IDS = 16
EARLY = (4, 7, 1, 2)
BEFORE_SECOND = (4, 7, 1, 2)
BEFORE_THIRD = ()
MIB = 1024 * 1024

F32 = jnp.float32
BF16 = jnp.bfloat16
ANY = pl.BlockSpec(memory_space=pl.ANY)
VMEM = pl.BlockSpec(memory_space=pltpu.VMEM)
SMEM = pl.BlockSpec(memory_space=pltpu.SMEM)


def params(mebibytes):
    return pltpu.CompilerParams(vmem_limit_bytes=mebibytes * MIB)


def cost(micros):
    return pl.CostEstimate(flops=0, bytes_accessed=int(micros * 3.5e6), transcendentals=0)


def shape(dims, dtype=BF16):
    return jax.ShapeDtypeStruct(dims, dtype)


def far(array):
    return pltpu.with_memory_space_constraint(array, pltpu.HBM)


def near(arrays):
    return [pltpu.with_memory_space_constraint(array, pltpu.VMEM) for array in arrays]


def ring_at(place, count):
    place = place % count
    return jnp.where(place < count // 2, 2 * place, 2 * (count - 1 - place) + 1)


def ring_place(index, count):
    return jnp.where(index % 2 == 0, index // 2, count - 1 - index // 2)


def ring_routes(count):
    order = [*range(0, count, 2), *range(count - 1, 0, -2)]
    onward = [(order[i], order[(i + 1) % count]) for i in range(count)]
    return onward, [(b, a) for a, b in onward]


def shift(block, axis, distance):
    count = lax.axis_size(axis)
    return lax.ppermute(block, axis, [(i, (i + distance) % count) for i in range(count)])


def swap(block, axis):
    return lax.ppermute(block, axis, [(0, 1), (1, 0)])


def tie(block, *others):
    return lax.optimization_barrier((block, *others))[0]


def first_part(t):
    return t * 11 // 16 // 8 * 8


def flip(block, axis, bit):
    return lax.ppermute(block, axis, [(i, i ^ bit) for i in range(lax.axis_size(axis))])


def ring_step(left, right, axis):
    onward, back = ring_routes(lax.axis_size(axis))
    return lax.ppermute(left, axis, onward), lax.ppermute(right, axis, back)


def join_kernel(tokens, cotangent, both):
    t = tokens.shape[0]
    both[:t] = tokens[...]
    both[t:] = cotangent[...]


def join(tokens, cotangent):
    t, width = tokens.shape
    return pl.pallas_call(
        join_kernel,
        out_shape=shape((2 * t, width)),
        in_specs=[VMEM] * 2,
        out_specs=VMEM,
        compiler_params=params(56),
        name="join",
        cost_estimate=cost(2),
    )(tokens, cotangent)


def pack_kernel(grid, gd, ud, dd, gr, ur, dr, gate, up, down, after, *refs):
    own = refs[0]
    sends = refs[1:SPREAD]
    slab, ids, used = refs[SPREAD:]
    me = lax.axis_index("fsdp")
    quarter = 2 * lax.axis_index("groups") + lax.axis_index("section")
    rows = BLK // 4
    slab[...] = jnp.zeros_like(slab)
    own[...] = jnp.zeros_like(own)
    ids[...] = jnp.zeros_like(ids)
    for kind, (dest, row_ids, blocks) in enumerate(((gd, gr, gate), (ud, ur, up), (dd, dr, down))):
        for offset in range(SPREAD):
            used[offset] = 0

        def place(j, carry, kind=kind, dest=dest, row_ids=row_ids, blocks=blocks):
            offset = dest[j]
            if grid:
                offset = me ^ lax.rem(me - offset + SPREAD, SPREAD)
            rank = used[offset]
            used[offset] = rank + 1
            slot = kind * CAP + rank
            start = pl.multiple_of(quarter * rows, rows)
            slab[offset, slot] = blocks[j, pl.ds(start, rows), :]
            ids[offset, pl.ds(slot, 1), :] = jnp.full((1, BLK), row_ids[j].astype(F32), F32)

            @pl.when(offset == 0)
            def _():
                for part in range(4):
                    rows_of = pl.ds(pl.multiple_of(slot * PART, PART), PART)
                    own[part, rows_of, :] = blocks[j, part * PART : (part + 1) * PART, :]

            return carry

        lax.fori_loop(0, blocks.shape[0], place, 0)
    for offset in range(1, SPREAD):
        sends[offset - 1][0 : PER * PART] = slab[offset].reshape(PER * PART, BLK)
        sends[offset - 1][PER * PART :] = ids[offset].astype(BF16)
    own[0, PER * PART :] = ids[0].astype(BF16)


def pack(grid, dests, row_ids, blocks, after):
    rows = BLK // 4
    return pl.pallas_call(
        functools.partial(pack_kernel, grid),
        out_shape=[shape((4, PER * PART + IDS, BLK))] + [shape((PER * PART + IDS, BLK))] * (SPREAD - 1),
        in_specs=[SMEM] * 6 + [VMEM] * 3 + [ANY],
        out_specs=[VMEM] * SPREAD,
        scratch_shapes=[
            pltpu.VMEM((SPREAD, PER, rows, BLK), BF16),
            pltpu.VMEM((SPREAD, IDS, BLK), F32),
            pltpu.SMEM((SPREAD,), jnp.int32),
        ],
        compiler_params=params(56),
        name="pack",
        cost_estimate=cost(3),
    )(*dests, *row_ids, *blocks, after)


def forward_kernel(layout, tokens_here, split, own, w0, w1, w2, w3, *refs):
    count = len(layout)
    shards = refs[:count]
    refs = refs[count:]
    field_out, hidden_out = refs[0], refs[1]
    outs = refs[2 : 3 + 3 * split]
    field, weights, id_rows, id_ints, id_scalars, left, total, shard_sems, sems = refs[3 + 3 * split :]
    width = field.shape[2]
    per_piece = width // BLK
    t = tokens_here
    axis_size = lax.axis_size("fsdp")
    me = lax.axis_index("fsdp")
    group = lax.axis_index("groups")
    section = lax.axis_index("section")
    quarters = (
        2 * group + section,
        2 * group + 1 - section,
        2 * (1 - group) + section,
        2 * (1 - group) + 1 - section,
    )

    own_copies = [
        pltpu.make_async_copy(own.at[:, 0 : PER * PART], weights.at[0], sems.at[0]),
        pltpu.make_async_copy(own.at[0, PER * PART :], id_rows.at[0], sems.at[1]),
        pltpu.make_async_copy(w0.at[:, PER * PART :], id_rows.at[1:SPREAD], sems.at[2]),
    ]
    weight_copies = []
    for n, ref in enumerate((w0, w1, w2, w3)):
        weight_copies.append(
            pltpu.make_async_copy(
                ref.at[:, 0 : PER * PART], weights.at[1:SPREAD, quarters[n]], sems.at[3 + n]
            )
        )
    shard_copies = []
    for n, (steps, first, length) in enumerate(layout):
        piece = ring_at(ring_place(me, axis_size) + steps, axis_size) if split else 0
        shard_copies.append(
            pltpu.make_async_copy(
                shards[n], field.at[piece, first : first + length], shard_sems.at[n]
            )
        )
    for copy in own_copies + shard_copies + weight_copies:
        copy.start()
    total[...] = jnp.zeros_like(total)
    for copy in own_copies[1:]:
        copy.wait()
    id_ints[...] = id_rows[...].astype(F32).astype(jnp.int32)
    id_copy = pltpu.make_async_copy(id_ints, id_scalars, sems.at[7])
    id_copy.start()
    for copy in shard_copies:
        copy.wait()
    field_copy = pltpu.make_async_copy(field, field_out, sems.at[8])
    field_copy.start()
    id_copy.wait()

    def where(offset, kind, rank):
        row = id_scalars[offset, kind * CAP + rank, 0]
        return row // per_piece, pl.multiple_of((row % per_piece) * BLK, BLK)

    for kind in range(KINDS):
        first = t if kind == 2 else 0
        for offset in range(SPREAD):
            for rank in range(CAP):
                piece, column = where(offset, kind, rank)
                n = offset * CAP + rank
                left[kind, :, n * BLK : (n + 1) * BLK] = field[
                    piece, first : first + t, pl.ds(column, BLK)
                ]
    own_copies[0].wait()
    for copy in weight_copies:
        copy.wait()

    def block(offset, slot):
        rows = slice(slot * PART, (slot + 1) * PART)
        return jnp.concatenate([weights[offset, part, rows] for part in range(4)], axis=0)

    def block_group(kind, offsets=range(SPREAD)):
        slots = range(kind * CAP, (kind + 1) * CAP)
        return [block(offset, slot) for offset in offsets for slot in slots]

    gate = jnp.dot(left[0], jnp.concatenate(block_group(0), axis=0), preferred_element_type=F32)
    upper = jnp.dot(left[1], jnp.concatenate(block_group(1), axis=0), preferred_element_type=F32)
    nt = (((1,), (1,)), ((), ()))
    across = jnp.concatenate(block_group(2), axis=1)
    hidden_grad = lax.dot_general(left[2], across, nt, preferred_element_type=F32)
    sigma = 1.0 / (1.0 + jnp.exp(-gate))
    hidden = (gate * sigma * upper).astype(BF16)
    gate_d = (hidden_grad * upper * sigma * (1.0 + gate * (1.0 - sigma))).astype(BF16)
    up_d = (hidden_grad * gate * sigma).astype(BF16)
    hidden_out[0] = gate_d
    hidden_out[1] = up_d
    hidden_out[2] = hidden
    for kind, grad in ((0, gate_d), (1, up_d)):
        for offset in range(SPREAD):
            terms = lax.dot_general(
                grad,
                jnp.concatenate(block_group(kind, [offset]), axis=0),
                nt,
                preferred_element_type=F32,
            )
            for rank in range(CAP):
                piece, column = where(offset, kind, rank)
                total[piece, :, pl.ds(column, BLK)] += terms[:, rank * BLK : (rank + 1) * BLK]
    if split:
        h = first_part(t)
        send_a, send_b, keep_a, keep_b = outs
        for high in range(2):
            for low in range(2):
                a = me ^ (2 * high + 4 * low)
                b = me ^ (4 * high + low)
                n = 2 * high + low
                send_a[n] = total[a ^ 1, :h].astype(BF16)
                keep_a[n] = total[a, :h].astype(BF16)
                send_b[n] = total[b ^ 2, h:].astype(BF16)
                keep_b[n] = total[b, h:].astype(BF16)
    else:
        outs[0][...] = total[...].astype(BF16)
    field_copy.wait()


def forward(own, quarters, pieces, split, piece_count):
    layout = [(steps, first, block.shape[0]) for block, steps, first in pieces]
    t = pieces[0][0].shape[0] // 2
    width = pieces[0][0].shape[1]
    if split:
        rows = first_part(t), t - first_part(t)
        outs = [shape((piece_count // 2, rows[n % 2], width)) for n in range(4)]
    else:
        outs = [shape((piece_count, t, width))]
    field = (piece_count, 2 * t, width)
    return pl.pallas_call(
        functools.partial(forward_kernel, layout, t, int(split)),
        out_shape=[shape(field), shape((KINDS, t, BLK))] + outs,
        in_specs=[ANY] * (5 + len(pieces)),
        out_specs=[ANY] + [VMEM] * (1 + len(outs)),
        scratch_shapes=[
            pltpu.VMEM(field, BF16),
            pltpu.VMEM((SPREAD, 4, PER * PART, BLK), BF16),
            pltpu.VMEM((SPREAD, IDS, BLK), BF16),
            pltpu.VMEM((SPREAD, IDS, BLK), jnp.int32),
            pltpu.SMEM((SPREAD, IDS, BLK), jnp.int32),
            pltpu.VMEM((KINDS, t, SPREAD * CAP * BLK), BF16),
            pltpu.VMEM((piece_count, t, width), F32),
            pltpu.SemaphoreType.DMA((len(pieces),)),
            pltpu.SemaphoreType.DMA((9,)),
        ],
        compiler_params=params(32),
        name="forward",
        cost_estimate=cost(8),
    )(far(own), *(near if split else list)([*quarters, *[block for block, _, _ in pieces]]))


def grads_kernel(layout, grid, gd, ud, dd, gr, ur, dr, field, *refs):
    out, columns, sems = refs[-3:]
    axis_size = lax.axis_size("fsdp")
    me = lax.axis_index("fsdp")
    t = field.shape[1] // 2
    per_piece = field.shape[2] // BLK
    copies = []
    for n, (array, row, away) in enumerate(layout):
        offset = (me - (me ^ away) + axis_size) % axis_size if grid else away
        copies.append(
            pltpu.make_async_copy(refs[array].at[row], columns.at[offset], sems.at[n])
        )
    for copy in copies:
        copy.start()
    for copy in copies:
        copy.wait()
    tn = (((0,), (0,)), ((), ()))
    slots = gd.shape[0]
    for kind, (dest, row_ids) in enumerate(((gd, gr), (ud, ur), (dd, dr))):
        first = t if kind == 2 else 0

        def one(j, carry, kind=kind, dest=dest, row_ids=row_ids, first=first):
            row = row_ids[j]
            column = pl.multiple_of((row % per_piece) * BLK, BLK)
            part = field[row // per_piece, first : first + t, pl.ds(column, BLK)]
            side = columns[dest[j], kind * t : (kind + 1) * t, :]
            pair_of = (side, part) if kind == 2 else (part, side)
            out[kind * slots + j] = lax.dot_general(
                *pair_of, tn, preferred_element_type=F32
            ).astype(BF16)
            return carry

        lax.fori_loop(0, slots, one, 0, unroll=16)


def grads(dests, row_ids, field, arrived, layout, grid, after):
    rows = arrived[0].shape[1]
    slots = dests[0].shape[0]
    return pl.pallas_call(
        functools.partial(grads_kernel, layout, grid),
        out_shape=shape((KINDS * slots, BLK, BLK)),
        in_specs=[SMEM] * 2 * KINDS + [VMEM] + [ANY] * (len(arrived) + len(after)),
        out_specs=VMEM,
        scratch_shapes=[
            pltpu.VMEM((SPREAD, rows, BLK), BF16),
            pltpu.SemaphoreType.DMA((SPREAD,)),
        ],
        compiler_params=params(32),
        name="grads",
        cost_estimate=cost(7.5),
    )(*dests, *row_ids, field, *arrived, *after)


def added(part, slots):
    other = swap(part, "section")
    summed = part.astype(F32) + other.astype(F32)
    return [summed[kind * slots : (kind + 1) * slots] for kind in range(KINDS)]


def shards(
    tokens,
    cotangent,
    gate_blocks,
    up_blocks,
    down_blocks,
    gate_dest,
    up_dest,
    down_dest,
    gate_rows,
    up_rows,
    down_rows,
):
    count = lax.axis_size("fsdp")
    grid = count == SPREAD and tokens.shape[1] % BLK == 0
    t = tokens.shape[0]
    slots = gate_blocks.shape[0]
    dests = [target[:, 0] for target in (gate_dest, up_dest, down_dest)]
    row_ids = [gate_rows, up_rows, down_rows]

    both = join(tokens, cotangent)
    own, *sends = pack(grid, dests, row_ids, (gate_blocks, up_blocks, down_blocks), both)
    if grid:
        slabs = {}
        steps = [ring_step(both, both, "fsdp")]
        for bits in EARLY:
            slabs[bits] = flip(sends[bits - 1], "fsdp", bits)
        held = lax.optimization_barrier((*steps[0], *[slabs[bits] for bits in BEFORE_SECOND]))
        steps.append(ring_step(*held[:2], "fsdp"))
        for bits in range(1, SPREAD):
            if bits not in EARLY:
                slabs[bits] = flip(tie(sends[bits - 1], *steps[0]), "fsdp", bits)
        held = lax.optimization_barrier((*steps[1], *[slabs[bits] for bits in BEFORE_THIRD]))
        steps.append(ring_step(*held[:2], "fsdp"))
        left, right = steps[2]
        steps.append(ring_step(left[:t], right[t:], "fsdp"))
        pieces = [(both, 0, 0)]
        for step, (left, right) in enumerate(steps, 1):
            pieces += [(left, -step, 0), (right, step, t if step == count // 2 else 0)]
        slabs = [slabs[bits] for bits in range(1, SPREAD)]
        slabs = lax.optimization_barrier((*slabs, *steps[1]))[:-2]
        piece_count = count
    else:
        pieces = [(lax.all_gather(both, "fsdp", axis=1, tiled=True), 0, 0)]
        slabs = [shift(block, "fsdp", -d) for d, block in enumerate(sends, 1)]
        piece_count = 1

    mine = jnp.stack(slabs, axis=0)
    across = swap(mine, "groups")
    beside = swap(mine, "section")
    diagonal = swap(across, "section")
    quarters = (mine, beside, across, diagonal)
    field, columns, *partial_input = forward(own, quarters, pieces, grid, piece_count)
    flat = columns.reshape(1, KINDS * t, BLK)

    if grid:
        send_a, send_b, keep_a, keep_b = partial_input
        got_a = flip(send_a, "fsdp", 1)
        two = jnp.concatenate([flat, flip(flat, "fsdp", 4)], axis=0)
        got_b = flip(tie(send_b, two), "fsdp", 2)
        beside = flip(two, "fsdp", 2)
        sum_a = keep_a + got_a
        away_a = tie(sum_a[2:])
        got_a = flip(away_a, "fsdp", 2)
        beside, away_a, got_b = lax.optimization_barrier((beside, away_a, got_b))
        four = jnp.concatenate([two, beside], axis=0)
        rest = flip(four, "fsdp", 1)
        sum_b = keep_b + got_b
        away_b = tie(sum_b[2:])
        got_b = flip(away_b, "fsdp", 4)
        arrived = [four, rest]
        layout = [(n, row, n + bits) for n in range(2) for row, bits in enumerate((0, 4, 2, 6))]
        part = grads(dests, row_ids, field, arrived, layout, grid, [away_a, away_b])
        got_a, part = lax.optimization_barrier((got_a, part))
        sum_a = sum_a[:2] + got_a
        away_a = tie(sum_a[1:])
        part, got_b, away_a = lax.optimization_barrier((part, got_b, away_a))
        got_a = flip(away_a, "fsdp", 4)
        sum_b = sum_b[:2] + got_b
        got_b = flip(sum_b[1:], "fsdp", 1)
        block_grads = added(part, slots)
        got_a, got_b, *block_grads = lax.optimization_barrier((got_a, got_b, *block_grads))
        input_grad = jnp.concatenate([sum_a[0] + got_a[0], sum_b[0] + got_b[0]], axis=0)
    else:
        input_grad = lax.psum_scatter(
            partial_input[0].reshape(t, -1), "fsdp", scatter_dimension=1, tiled=True
        )
        arrived = [flat] + [shift(flat, "fsdp", d) for d in range(1, SPREAD)]
        layout = [(d, 0, d) for d in range(SPREAD)]
        part = grads(dests, row_ids, field, arrived, layout, grid, [])
        block_grads = added(part, slots)
    return input_grad, *block_grads


def solution(mesh):
    return jax.shard_map(
        shards,
        mesh=mesh,
        in_specs=(
            P(("groups", "section"), "fsdp"),
            P(("groups", "section"), "fsdp"),
            P("fsdp", None, None),
            P("fsdp", None, None),
            P("fsdp", None, None),
            P("fsdp", None),
            P("fsdp", None),
            P("fsdp", None),
            P("fsdp"),
            P("fsdp"),
            P("fsdp"),
        ),
        out_specs=(
            P(("groups", "section"), "fsdp"),
            P(("groups", "fsdp"), None, None),
            P(("groups", "fsdp"), None, None),
            P(("groups", "fsdp"), None, None),
        ),
        check_vma=False,
    )
```

```python
import functools

import jax
import jax.numpy as jnp
from jax import lax
from jax.experimental import pallas as pl
from jax.experimental.pallas import tpu as pltpu
from jax.sharding import PartitionSpec as P

BLK = 128
SPREAD = 8
CAP = 3
KINDS = 3
PER = KINDS * CAP
PART = BLK // 4
IDS = 16
EARLY = (4, 7, 1, 2)
BEFORE_SECOND = (4, 7, 1, 2)
BEFORE_THIRD = ()
MIB = 1024 * 1024

F32 = jnp.float32
BF16 = jnp.bfloat16
ANY = pl.BlockSpec(memory_space=pl.ANY)
VMEM = pl.BlockSpec(memory_space=pltpu.VMEM)
SMEM = pl.BlockSpec(memory_space=pltpu.SMEM)


def params(mebibytes):
    return pltpu.CompilerParams(vmem_limit_bytes=mebibytes * MIB)


def cost(micros):
    return pl.CostEstimate(flops=0, bytes_accessed=int(micros * 3.5e6), transcendentals=0)


def shape(dims, dtype=BF16):
    return jax.ShapeDtypeStruct(dims, dtype)


def far(array):
    return pltpu.with_memory_space_constraint(array, pltpu.HBM)


def near(arrays):
    return [pltpu.with_memory_space_constraint(array, pltpu.VMEM) for array in arrays]


def ring_at(place, count):
    place = place % count
    return jnp.where(place < count // 2, 2 * place, 2 * (count - 1 - place) + 1)


def ring_place(index, count):
    return jnp.where(index % 2 == 0, index // 2, count - 1 - index // 2)


def ring_routes(count):
    order = [*range(0, count, 2), *range(count - 1, 0, -2)]
    onward = [(order[i], order[(i + 1) % count]) for i in range(count)]
    return onward, [(b, a) for a, b in onward]


def shift(block, axis, distance):
    count = lax.axis_size(axis)
    return lax.ppermute(block, axis, [(i, (i + distance) % count) for i in range(count)])


def swap(block, axis):
    return lax.ppermute(block, axis, [(0, 1), (1, 0)])


def tie(block, *others):
    return lax.optimization_barrier((block, *others))[0]


def first_part(t):
    return t * 11 // 16 // 8 * 8


def flip(block, axis, bit):
    return lax.ppermute(block, axis, [(i, i ^ bit) for i in range(lax.axis_size(axis))])


def ring_step(left, right, axis):
    onward, back = ring_routes(lax.axis_size(axis))
    return lax.ppermute(left, axis, onward), lax.ppermute(right, axis, back)


def join_kernel(tokens, cotangent, both):
    t = tokens.shape[0]
    both[:t] = tokens[...]
    both[t:] = cotangent[...]


def join(tokens, cotangent):
    t, width = tokens.shape
    return pl.pallas_call(
        join_kernel,
        out_shape=shape((2 * t, width)),
        in_specs=[VMEM] * 2,
        out_specs=VMEM,
        compiler_params=params(56),
        name="join",
        cost_estimate=cost(2),
    )(tokens, cotangent)


def pack_kernel(grid, gd, ud, dd, gr, ur, dr, gate, up, down, after, *refs):
    own = refs[0]
    sends = refs[1:SPREAD]
    slab, ids, used = refs[SPREAD:]
    me = lax.axis_index("fsdp")
    quarter = 2 * lax.axis_index("groups") + lax.axis_index("section")
    rows = BLK // 4
    slab[...] = jnp.zeros_like(slab)
    own[...] = jnp.zeros_like(own)
    ids[...] = jnp.zeros_like(ids)
    for kind, (dest, row_ids, blocks) in enumerate(((gd, gr, gate), (ud, ur, up), (dd, dr, down))):
        for offset in range(SPREAD):
            used[offset] = 0

        def place(j, carry, kind=kind, dest=dest, row_ids=row_ids, blocks=blocks):
            offset = dest[j]
            if grid:
                offset = me ^ lax.rem(me - offset + SPREAD, SPREAD)
            rank = used[offset]
            used[offset] = rank + 1
            slot = kind * CAP + rank
            start = pl.multiple_of(quarter * rows, rows)
            slab[offset, slot] = blocks[j, pl.ds(start, rows), :]
            ids[offset, pl.ds(slot, 1), :] = jnp.full((1, BLK), row_ids[j].astype(F32), F32)

            @pl.when(offset == 0)
            def _():
                for part in range(4):
                    rows_of = pl.ds(pl.multiple_of(slot * PART, PART), PART)
                    own[part, rows_of, :] = blocks[j, part * PART : (part + 1) * PART, :]

            return carry

        lax.fori_loop(0, blocks.shape[0], place, 0)
    for offset in range(1, SPREAD):
        sends[offset - 1][0 : PER * PART] = slab[offset].reshape(PER * PART, BLK)
        sends[offset - 1][PER * PART :] = ids[offset].astype(BF16)
    own[0, PER * PART :] = ids[0].astype(BF16)


def pack(grid, dests, row_ids, blocks, after):
    rows = BLK // 4
    return pl.pallas_call(
        functools.partial(pack_kernel, grid),
        out_shape=[shape((4, PER * PART + IDS, BLK))] + [shape((PER * PART + IDS, BLK))] * (SPREAD - 1),
        in_specs=[SMEM] * 6 + [VMEM] * 3 + [ANY],
        out_specs=[VMEM] * SPREAD,
        scratch_shapes=[
            pltpu.VMEM((SPREAD, PER, rows, BLK), BF16),
            pltpu.VMEM((SPREAD, IDS, BLK), F32),
            pltpu.SMEM((SPREAD,), jnp.int32),
        ],
        compiler_params=params(56),
        name="pack",
        cost_estimate=cost(3),
    )(*dests, *row_ids, *blocks, after)


def forward_kernel(layout, tokens_here, split, own, w0, w1, w2, w3, *refs):
    count = len(layout)
    shards = refs[:count]
    refs = refs[count:]
    field_out, hidden_out = refs[0], refs[1]
    outs = refs[2 : 3 + 3 * split]
    field, weights, id_rows, id_ints, id_scalars, total, shard_sems, sems = refs[3 + 3 * split :]
    width = field.shape[2]
    per_piece = width // BLK
    t = tokens_here
    axis_size = lax.axis_size("fsdp")
    me = lax.axis_index("fsdp")
    group = lax.axis_index("groups")
    section = lax.axis_index("section")
    quarters = (
        2 * group + section,
        2 * group + 1 - section,
        2 * (1 - group) + section,
        2 * (1 - group) + 1 - section,
    )

    own_copies = [
        pltpu.make_async_copy(own.at[:, 0 : PER * PART], weights.at[0], sems.at[0]),
        pltpu.make_async_copy(own.at[0, PER * PART :], id_rows.at[0], sems.at[1]),
        pltpu.make_async_copy(w0.at[:, PER * PART :], id_rows.at[1:SPREAD], sems.at[2]),
    ]
    weight_copies = []
    for n, ref in enumerate((w0, w1, w2, w3)):
        weight_copies.append(
            pltpu.make_async_copy(
                ref.at[:, 0 : PER * PART], weights.at[1:SPREAD, quarters[n]], sems.at[3 + n]
            )
        )
    shard_copies = []
    for n, (steps, first, length) in enumerate(layout):
        piece = ring_at(ring_place(me, axis_size) + steps, axis_size) if split else 0
        shard_copies.append(
            pltpu.make_async_copy(
                shards[n], field.at[piece, first : first + length], shard_sems.at[n]
            )
        )
    for copy in own_copies + shard_copies + weight_copies:
        copy.start()
    total[...] = jnp.zeros_like(total)
    for copy in own_copies[1:]:
        copy.wait()
    id_ints[...] = id_rows[...].astype(F32).astype(jnp.int32)
    id_copy = pltpu.make_async_copy(id_ints, id_scalars, sems.at[7])
    id_copy.start()
    for copy in shard_copies:
        copy.wait()
    field_copy = pltpu.make_async_copy(field, field_out, sems.at[8])
    field_copy.start()
    id_copy.wait()

    def where(offset, kind, rank):
        row = id_scalars[offset, kind * CAP + rank, 0]
        return row // per_piece, pl.multiple_of((row % per_piece) * BLK, BLK)

    def left(kind):
        first = t if kind == 2 else 0
        parts = []
        for offset in range(SPREAD):
            for rank in range(CAP):
                piece, column = where(offset, kind, rank)
                parts.append(field[piece, first : first + t, pl.ds(column, BLK)])
        return jnp.concatenate(parts, axis=1)

    own_copies[0].wait()
    for copy in weight_copies:
        copy.wait()

    def block(offset, slot):
        rows = slice(slot * PART, (slot + 1) * PART)
        return jnp.concatenate([weights[offset, part, rows] for part in range(4)], axis=0)

    def block_group(kind, offsets=range(SPREAD)):
        slots = range(kind * CAP, (kind + 1) * CAP)
        return [block(offset, slot) for offset in offsets for slot in slots]

    gate = jnp.dot(left(0), jnp.concatenate(block_group(0), axis=0), preferred_element_type=F32)
    upper = jnp.dot(left(1), jnp.concatenate(block_group(1), axis=0), preferred_element_type=F32)
    nt = (((1,), (1,)), ((), ()))
    across = jnp.concatenate(block_group(2), axis=1)
    hidden_grad = lax.dot_general(left(2), across, nt, preferred_element_type=F32)
    sigma = 1.0 / (1.0 + jnp.exp(-gate))
    hidden = (gate * sigma * upper).astype(BF16)
    gate_d = (hidden_grad * upper * sigma * (1.0 + gate * (1.0 - sigma))).astype(BF16)
    up_d = (hidden_grad * gate * sigma).astype(BF16)
    hidden_out[0] = gate_d
    hidden_out[1] = up_d
    hidden_out[2] = hidden
    for kind, grad in ((0, gate_d), (1, up_d)):
        for offset in range(SPREAD):
            terms = lax.dot_general(
                grad,
                jnp.concatenate(block_group(kind, [offset]), axis=0),
                nt,
                preferred_element_type=F32,
            )
            for rank in range(CAP):
                piece, column = where(offset, kind, rank)
                total[piece, :, pl.ds(column, BLK)] += terms[:, rank * BLK : (rank + 1) * BLK]
    if split:
        h = first_part(t)
        send_a, send_b, keep_a, keep_b = outs
        for high in range(2):
            for low in range(2):
                a = me ^ (2 * high + 4 * low)
                b = me ^ (4 * high + low)
                n = 2 * high + low
                send_a[n] = total[a ^ 1, :h].astype(BF16)
                keep_a[n] = total[a, :h].astype(BF16)
                send_b[n] = total[b ^ 2, h:].astype(BF16)
                keep_b[n] = total[b, h:].astype(BF16)
    else:
        outs[0][...] = total[...].astype(BF16)
    field_copy.wait()


def forward(own, quarters, pieces, split, piece_count):
    layout = [(steps, first, block.shape[0]) for block, steps, first in pieces]
    t = pieces[0][0].shape[0] // 2
    width = pieces[0][0].shape[1]
    if split:
        rows = first_part(t), t - first_part(t)
        outs = [shape((piece_count // 2, rows[n % 2], width)) for n in range(4)]
    else:
        outs = [shape((piece_count, t, width))]
    field = (piece_count, 2 * t, width)
    return pl.pallas_call(
        functools.partial(forward_kernel, layout, t, int(split)),
        out_shape=[shape(field), shape((KINDS, t, BLK))] + outs,
        in_specs=[ANY] * (5 + len(pieces)),
        out_specs=[ANY] + [VMEM] * (1 + len(outs)),
        scratch_shapes=[
            pltpu.VMEM(field, BF16),
            pltpu.VMEM((SPREAD, 4, PER * PART, BLK), BF16),
            pltpu.VMEM((SPREAD, IDS, BLK), BF16),
            pltpu.VMEM((SPREAD, IDS, BLK), jnp.int32),
            pltpu.SMEM((SPREAD, IDS, BLK), jnp.int32),
            pltpu.VMEM((piece_count, t, width), F32),
            pltpu.SemaphoreType.DMA((len(pieces),)),
            pltpu.SemaphoreType.DMA((9,)),
        ],
        compiler_params=params(32),
        name="forward",
        cost_estimate=cost(8),
    )(far(own), *(near if split else list)([*quarters, *[block for block, _, _ in pieces]]))


def grads_kernel(layout, grid, gd, ud, dd, gr, ur, dr, field, *refs):
    out, columns, sems = refs[-3:]
    axis_size = lax.axis_size("fsdp")
    me = lax.axis_index("fsdp")
    t = field.shape[1] // 2
    per_piece = field.shape[2] // BLK
    copies = []
    for n, (array, row, away) in enumerate(layout):
        offset = (me - (me ^ away) + axis_size) % axis_size if grid else away
        copies.append(
            pltpu.make_async_copy(refs[array].at[row], columns.at[offset], sems.at[n])
        )
    for copy in copies:
        copy.start()
    for copy in copies:
        copy.wait()
    tn = (((0,), (0,)), ((), ()))
    slots = gd.shape[0]
    for kind, (dest, row_ids) in enumerate(((gd, gr), (ud, ur), (dd, dr))):
        first = t if kind == 2 else 0

        def one(j, carry, kind=kind, dest=dest, row_ids=row_ids, first=first):
            row = row_ids[j]
            column = pl.multiple_of((row % per_piece) * BLK, BLK)
            part = field[row // per_piece, first : first + t, pl.ds(column, BLK)]
            side = columns[dest[j], kind * t : (kind + 1) * t, :]
            pair_of = (side, part) if kind == 2 else (part, side)
            out[kind * slots + j] = lax.dot_general(
                *pair_of, tn, preferred_element_type=F32
            ).astype(BF16)
            return carry

        lax.fori_loop(0, slots, one, 0, unroll=16)


def grads(dests, row_ids, field, arrived, layout, grid, after):
    rows = arrived[0].shape[1]
    slots = dests[0].shape[0]
    return pl.pallas_call(
        functools.partial(grads_kernel, layout, grid),
        out_shape=shape((KINDS * slots, BLK, BLK)),
        in_specs=[SMEM] * 2 * KINDS + [VMEM] + [ANY] * (len(arrived) + len(after)),
        out_specs=VMEM,
        scratch_shapes=[
            pltpu.VMEM((SPREAD, rows, BLK), BF16),
            pltpu.SemaphoreType.DMA((SPREAD,)),
        ],
        compiler_params=params(32),
        name="grads",
        cost_estimate=cost(7.5),
    )(*dests, *row_ids, field, *arrived, *after)


def added(part, slots):
    other = swap(part, "section")
    summed = part.astype(F32) + other.astype(F32)
    return [summed[kind * slots : (kind + 1) * slots] for kind in range(KINDS)]


def shards(
    tokens,
    cotangent,
    gate_blocks,
    up_blocks,
    down_blocks,
    gate_dest,
    up_dest,
    down_dest,
    gate_rows,
    up_rows,
    down_rows,
):
    count = lax.axis_size("fsdp")
    grid = count == SPREAD and tokens.shape[1] % BLK == 0
    t = tokens.shape[0]
    slots = gate_blocks.shape[0]
    dests = [target[:, 0] for target in (gate_dest, up_dest, down_dest)]
    row_ids = [gate_rows, up_rows, down_rows]

    both = join(tokens, cotangent)
    own, *sends = pack(grid, dests, row_ids, (gate_blocks, up_blocks, down_blocks), both)
    if grid:
        slabs = {}
        steps = [ring_step(both, both, "fsdp")]
        for bits in EARLY:
            slabs[bits] = flip(sends[bits - 1], "fsdp", bits)
        held = lax.optimization_barrier((*steps[0], *[slabs[bits] for bits in BEFORE_SECOND]))
        steps.append(ring_step(*held[:2], "fsdp"))
        for bits in range(1, SPREAD):
            if bits not in EARLY:
                slabs[bits] = flip(tie(sends[bits - 1], *steps[0]), "fsdp", bits)
        held = lax.optimization_barrier((*steps[1], *[slabs[bits] for bits in BEFORE_THIRD]))
        steps.append(ring_step(*held[:2], "fsdp"))
        left, right = steps[2]
        steps.append(ring_step(left[:t], right[t:], "fsdp"))
        pieces = [(both, 0, 0)]
        for step, (left, right) in enumerate(steps, 1):
            pieces += [(left, -step, 0), (right, step, t if step == count // 2 else 0)]
        slabs = [slabs[bits] for bits in range(1, SPREAD)]
        slabs = lax.optimization_barrier((*slabs, *steps[1]))[:-2]
        piece_count = count
    else:
        pieces = [(lax.all_gather(both, "fsdp", axis=1, tiled=True), 0, 0)]
        slabs = [shift(block, "fsdp", -d) for d, block in enumerate(sends, 1)]
        piece_count = 1

    mine = jnp.stack(slabs, axis=0)
    across = swap(mine, "groups")
    beside = swap(mine, "section")
    diagonal = swap(across, "section")
    quarters = (mine, beside, across, diagonal)
    field, columns, *partial_input = forward(own, quarters, pieces, grid, piece_count)
    flat = columns.reshape(1, KINDS * t, BLK)

    if grid:
        send_a, send_b, keep_a, keep_b = partial_input
        got_a = flip(send_a, "fsdp", 1)
        two = jnp.concatenate([flat, flip(flat, "fsdp", 4)], axis=0)
        got_b = flip(tie(send_b, two), "fsdp", 2)
        beside = flip(two, "fsdp", 2)
        sum_a = keep_a + got_a
        away_a = tie(sum_a[2:])
        got_a = flip(away_a, "fsdp", 2)
        beside, away_a, got_b = lax.optimization_barrier((beside, away_a, got_b))
        four = jnp.concatenate([two, beside], axis=0)
        rest = flip(four, "fsdp", 1)
        sum_b = keep_b + got_b
        away_b = tie(sum_b[2:])
        got_b = flip(away_b, "fsdp", 4)
        arrived = [four, rest]
        layout = [(n, row, n + bits) for n in range(2) for row, bits in enumerate((0, 4, 2, 6))]
        part = grads(dests, row_ids, field, arrived, layout, grid, [away_a, away_b])
        got_a, part = lax.optimization_barrier((got_a, part))
        sum_a = sum_a[:2] + got_a
        away_a = tie(sum_a[1:])
        part, got_b, away_a = lax.optimization_barrier((part, got_b, away_a))
        got_a = flip(away_a, "fsdp", 4)
        sum_b = sum_b[:2] + got_b
        got_b = flip(sum_b[1:], "fsdp", 1)
        block_grads = added(part, slots)
        got_a, got_b, *block_grads = lax.optimization_barrier((got_a, got_b, *block_grads))
        input_grad = jnp.concatenate([sum_a[0] + got_a[0], sum_b[0] + got_b[0]], axis=0)
    else:
        input_grad = lax.psum_scatter(
            partial_input[0].reshape(t, -1), "fsdp", scatter_dimension=1, tiled=True
        )
        arrived = [flat] + [shift(flat, "fsdp", d) for d in range(1, SPREAD)]
        layout = [(d, 0, d) for d in range(SPREAD)]
        part = grads(dests, row_ids, field, arrived, layout, grid, [])
        block_grads = added(part, slots)
    return input_grad, *block_grads


def solution(mesh):
    return jax.shard_map(
        shards,
        mesh=mesh,
        in_specs=(
            P(("groups", "section"), "fsdp"),
            P(("groups", "section"), "fsdp"),
            P("fsdp", None, None),
            P("fsdp", None, None),
            P("fsdp", None, None),
            P("fsdp", None),
            P("fsdp", None),
            P("fsdp", None),
            P("fsdp"),
            P("fsdp"),
            P("fsdp"),
        ),
        out_specs=(
            P(("groups", "section"), "fsdp"),
            P(("groups", "fsdp"), None, None),
            P(("groups", "fsdp"), None, None),
            P(("groups", "fsdp"), None, None),
        ),
        check_vma=False,
    )
```
